512 devices in a mesh: row: 16 (over z_hi, x), col: 32 (over z_lo, y, core).
Axes of the slice: x: 4, y: 8, z: 8 (z_hi: 4, z_lo: 2; z = z_hi * 2 + z_lo), core: 2. Of those that a mesh axis runs over, the one named last changes fastest.
Arguments:
- samples: bfloat16 [32768, 64], P(('row', 'col')), may hold values from -6 to 6
- scores: bfloat16 [32768, 64], P(('row', 'col')), may hold values from -6 to 6
- tile_groups: int32 [16, 32], P('row', 'col'), may hold values from 1 to 8, as said below
Outputs:
- grad_samples: float32 [32768, 64], P(('row', 'col'))
- grad_scores: float32 [32768, 64], P(('row', 'col'))
- loss: float32 [], replicated
The draws below stay inside these ranges and needn't reach their ends.
Inputs may be any that keep to these rules, and one draw needn't show every extreme that they name: `tile_groups`: the number of column groups of 128 samples that each tile uses, counted from the start of its column block; the value 8 occurs in every draw.
All inputs are finite; a program needn't handle non-finite values.
Results may differ from the reference program's by a relative error of at most 0.0011.
Values may be sent and summed in bfloat16 or wider, within the bound.
A program may use at most 64 MiB of HBM per device.

```python
import jax
import jax.numpy as jnp
from jax import lax

D = 64
SAMPLES_DEV = 64
SPAN = 128
SAMPLES = 32768
GROUPS = 8
N_ROW = 16
N_COL = 32


def draw_tile_groups(key, part):
    key = jax.random.fold_in(key, 7)
    first, second = jax.random.split(key)
    values = jax.random.randint(first, (N_ROW * N_COL,), 1, GROUPS + 1).astype(jnp.int32)
    where = jax.random.randint(second, (), 0, N_ROW * N_COL)
    values = values.at[where].set(GROUPS)
    return values.reshape(N_ROW, N_COL)


def draw_samples(key, part):
    key = jax.random.fold_in(key, 11)
    dir_key, coef_key, noise_key = jax.random.split(key, 3)
    directions = jax.random.normal(dir_key, (4, D), jnp.float32)
    weights = 0.5 * jax.random.normal(coef_key, (SAMPLES, 4), jnp.float32)
    noise = jax.random.normal(noise_key, (SAMPLES, D), jnp.float32)
    values = noise
    for index in range(4):
        values = values + weights[:, index:index + 1] * directions[index:index + 1, :]
    values = jnp.clip(values, -6.0, 6.0)
    return values.astype(jnp.bfloat16)


def shard_levels(own_key, extent, cuts, low, top_value):
    loudness, own = 1.0, jax.random.fold_in(own_key, 6)
    for position, parts in cuts:
        heights = jnp.exp(jax.random.uniform(jax.random.fold_in(own, position), (parts,), jnp.float32, low / len(cuts), top_value / len(cuts)))
        loudness = loudness * jnp.repeat(heights, extent[position] // parts).reshape([-1 if axis == position else 1 for axis in range(len(extent))])
    return loudness


def centred(own_key, extent, scale, reach, cuts=(), held_as=jnp.bfloat16):
    entries = scale * jax.random.normal(own_key, extent, jnp.float32)
    if cuts:
        entries = entries * shard_levels(own_key, extent, cuts, -0.22, 0.18)
    return jnp.clip(entries, -reach, reach).astype(held_as)


def setup_inputs(seed: int = 0) -> dict:
    keys = jax.random.split(jax.random.key(seed), 4)
    samples = draw_samples(jax.random.fold_in(keys[3], 71), 0)
    scores = centred(keys[1], (SAMPLES, D), 1.0, 6.0, ((0, 512),))
    tile_groups = draw_tile_groups(jax.random.fold_in(keys[3], 71), 0)
    return dict(samples=samples, scores=scores, tile_groups=tile_groups)


def tile_terms(rows, cols, active, row_index, col_index, m_dev, offset):
    width = rows.shape[1] // 2
    h_two = float(width)
    x_rows = rows[:, :width]
    s_rows = rows[:, width:]
    x_cols = cols[:, :width]
    s_cols = cols[:, width:]
    g_xx = jnp.dot(x_rows, x_cols.T, preferred_element_type=jnp.float32)
    g_xs = jnp.dot(x_rows, s_cols.T, preferred_element_type=jnp.float32)
    g_sx = jnp.dot(s_rows, x_cols.T, preferred_element_type=jnp.float32)
    g_ss = jnp.dot(s_rows, s_cols.T, preferred_element_type=jnp.float32)
    xr32 = x_rows.astype(jnp.float32)
    sr32 = s_rows.astype(jnp.float32)
    xc32 = x_cols.astype(jnp.float32)
    sc32 = s_cols.astype(jnp.float32)
    norm_rows = jnp.sum(xr32 * xr32, axis=1)
    norm_cols = jnp.sum(xc32 * xc32, axis=1)
    self_rows = jnp.sum(xr32 * sr32, axis=1)
    self_cols = jnp.sum(xc32 * sc32, axis=1)
    dist = norm_rows[:, None] + norm_cols[None, :] - 2.0 * g_xx
    kernel = jnp.exp(-dist / (2.0 * h_two))
    stein = g_ss + (self_rows[:, None] - g_sx - g_xs + self_cols[None, :]) / h_two + width / h_two - dist / (h_two * h_two)
    row_pos = jnp.arange(rows.shape[0], dtype=jnp.int32)[:, None]
    col_pos = jnp.arange(cols.shape[0], dtype=jnp.int32)[None, :] + offset
    local_row = row_pos - col_index * m_dev
    local_col = col_pos - row_index * m_dev
    diagonal = (local_row == local_col) & (local_row >= 0) & (local_row < m_dev)
    keep = (col_pos // SPAN < active) & jnp.logical_not(diagonal)
    kept = jnp.where(keep, kernel, jnp.float32(0.0))
    loss = jnp.sum(kept * stein)
    count = jnp.sum(keep.astype(jnp.float32))
    coef = kept * (stein / h_two + 2.0 / (h_two * h_two))
    kept_half = kept.astype(jnp.bfloat16)
    coef_half = coef.astype(jnp.bfloat16)
    ksum_rows = jnp.sum(kept, axis=1)[:, None]
    csum_rows = jnp.sum(coef, axis=1)[:, None]
    ksum_cols = jnp.sum(kept, axis=0)[:, None]
    csum_cols = jnp.sum(coef, axis=0)[:, None]
    k_cols = jnp.dot(kept_half, cols, preferred_element_type=jnp.float32)
    a_cols = jnp.dot(coef_half, x_cols, preferred_element_type=jnp.float32)
    dims = (((0,), (0,)), ((), ()))
    k_rows = lax.dot_general(kept_half, rows, dims, preferred_element_type=jnp.float32)
    a_rows = lax.dot_general(coef_half, x_rows, dims, preferred_element_type=jnp.float32)
    row_gx = a_cols - xr32 * csum_rows + (sr32 * ksum_rows - k_cols[:, width:]) / h_two
    row_gs = k_cols[:, width:] + (xr32 * ksum_rows - k_cols[:, :width]) / h_two
    col_gx = a_rows - xc32 * csum_cols - (k_rows[:, width:] - sc32 * ksum_cols) / h_two
    col_gs = k_rows[:, width:] - (k_rows[:, :width] - xc32 * ksum_cols) / h_two
    row_grad = jnp.concatenate([row_gx, row_gs], axis=1)
    col_grad = jnp.concatenate([col_gx, col_gs], axis=1)
    return loss, count, row_grad, col_grad


def reference(samples, scores, tile_groups):
    pair = jnp.concatenate([samples, scores], axis=1)
    blocks = pair.reshape(N_ROW, N_COL, SAMPLES_DEV, 2 * D)
    start = jnp.zeros((N_ROW, N_COL, SAMPLES_DEV, 2 * D), jnp.float32)

    def visit(carry, tile):
        loss_sum, count_sum, grads = carry
        row_index = (tile // N_COL).astype(jnp.int32)
        col_index = (tile % N_COL).astype(jnp.int32)
        rows = blocks[row_index].reshape(N_COL * SAMPLES_DEV, 2 * D)
        cols = blocks[:, col_index].reshape(N_ROW * SAMPLES_DEV, 2 * D)
        active = tile_groups[row_index, col_index]
        loss, count, row_grad, col_grad = tile_terms(rows, cols, active, row_index, col_index, SAMPLES_DEV, 0)
        grads = grads.at[row_index].add(row_grad.reshape(N_COL, SAMPLES_DEV, 2 * D))
        grads = grads.at[:, col_index].add(col_grad.reshape(N_ROW, SAMPLES_DEV, 2 * D))
        return (loss_sum + loss, count_sum + count, grads), None

    init = (jnp.float32(0.0), jnp.float32(0.0), start)
    tiles = jnp.arange(N_ROW * N_COL, dtype=jnp.int32)
    (loss_sum, count_sum, grads), _ = lax.scan(visit, init, tiles)
    scale = jnp.float32(SAMPLES) / count_sum
    grads = grads.reshape(SAMPLES, 2 * D) * scale
    return grads[:, :D], grads[:, D:], loss_sum / count_sum
```

```python
import jax
import ml_dtypes
import jax.numpy as jnp
from jax import lax
from jax.experimental import pallas as pl
from jax.experimental.pallas import tpu as pltpu
from jax.sharding import PartitionSpec as P

MESH = pl.DeviceIdType.MESH
F32 = jnp.float32
BF16 = jnp.bfloat16

NROW, NCOL = 16, 32
M = 64
CHUNKS = 9
RG = 2 * CHUNKS
SUPER = 3
RS_GROUPS = RG // SUPER
RROWS = RS_GROUPS * M
QUART = 4
QCOLS = 4 * M
EVERYONE = float(M * NROW * NCOL)
BIG = -16384.0

OFFSETS = (
    (0, 4, True), (0, 3, False), (1, -3, False),
    (1, None, False), (1, 2, False), (0, -2, False),
    (0, 1, False), (1, -1, False), (0, 0, True),
)


def split3(value):
    hi = value.astype(BF16).astype(F32)
    rest = value - hi
    mid = rest.astype(BF16).astype(F32)
    return hi, mid, rest - mid


def dot(a, b):
    return lax.dot_general(a, b, (((1,), (0,)), ((), ())), preferred_element_type=F32)


def dot_nt(a, b):
    return lax.dot_general(a, b, (((1,), (1,)), ((), ())), preferred_element_type=F32)


def lanes(rows=1, width=128):
    return lax.broadcasted_iota(jnp.int32, (rows, width), 1)


def squares(p, sw):
    q = p * jnp.where(lanes() < 64, p, sw)
    hi = q.astype(BF16)
    return jnp.concatenate([hi, (q - hi.astype(F32)).astype(BF16)], axis=1)


def sum_weights(e_lanes, s_lanes):
    k = lax.broadcasted_iota(jnp.int32, (256, 128), 0) % 128
    lane = lax.broadcasted_iota(jnp.int32, (256, 128), 1)
    is_x = k < 64
    out = jnp.zeros((256, 128), F32)
    if e_lanes is not None:
        in_e = (lane >= e_lanes) & (lane < e_lanes + 3)
        out = jnp.where(in_e & is_x, -(2.0 ** -7), out)
    if s_lanes is not None:
        in_s = (lane >= s_lanes) & (lane < s_lanes + 3)
        out = jnp.where(in_s, jnp.where(is_x, -(2.0 ** -18), 2.0 ** -12), out)
    return out.astype(BF16)


def pick3(value):
    hi, mid, lo = split3(value)
    part = lanes() % 3
    return jnp.where(part == 0, hi, jnp.where(part == 1, mid, lo))


def prep_rows(ref, step):
    pair = ref.rowbuf[pl.ds(step * RS_GROUPS, RS_GROUPS)].reshape(RROWS, 128)
    p = pair.astype(F32)
    sw = pltpu.roll(p, 64, 1)
    lane = lanes(RROWS)
    group = lax.broadcasted_iota(jnp.int32, (RROWS, 128), 0) // M + step * RS_GROUPS
    sums = dot(squares(p, sw), sum_weights(0, 6))
    one = ((lane >= 3) & (lane < 6)) | (lane == 9)
    one = one | (lane == 10 + group) | (lane == 10 + RG + group) | (lane == 10 + 2 * RG + group)
    misc = pick3(sums) + one.astype(F32)
    ext = jnp.where(lane < 64, misc, p).astype(BF16)
    ref.a_op[pl.ds(step * RROWS, RROWS), :] = jnp.concatenate([pair, ext], axis=1)
    pt = p.T
    xt, st = pt[0:64], pt[64:128]
    ones = jnp.ones((16, RROWS), F32)
    ref.f1t[step] = jnp.concatenate([st * (-1.0 / 64), st, xt * (-1.0 / 64), ones], axis=0).astype(BF16)
    ref.f2t[step] = jnp.concatenate([xt, ones], axis=0).astype(BF16)


def prep_cols(ref, quarter):
    pair = ref.colbuf[pl.ds(quarter * 4, 4)].reshape(QCOLS, 128)
    p = pair.astype(F32)
    sw = pltpu.roll(p, 64, 1)
    lane = lanes()
    first = lane < 64
    sq = squares(p, sw)
    sums_e = dot(sq, sum_weights(3, None))
    sums_s = dot(sq, sum_weights(None, 3))
    u = p * jnp.where(first, 2.0 ** -17, 2.0 ** -6) - sw * (2.0 ** -12)
    u_hi = u.astype(BF16)
    e1 = jnp.where(first, p * (1.0 / 64), 0.0).astype(BF16)
    e2 = pick3(sums_e) + (lane < 3).astype(F32)
    s2 = pick3(sums_s) + ((lane >= 6) & (lane < 9)).astype(F32) + jnp.where(lane == 9, 33.0 / 2048, 0.0)
    s2 = jnp.where(first, s2, u - u_hi.astype(F32))
    ref.b_op[quarter, 0:QCOLS, :] = jnp.concatenate([e1, e2.astype(BF16)], axis=1)
    ref.b_op[quarter, QCOLS:2 * QCOLS, :] = jnp.concatenate([u_hi, s2.astype(BF16)], axis=1)
    sw64 = sw * (-1.0 / 64)
    f1a = jnp.where(first, sw64, p)
    f1b = jnp.where(first, (lane == 0).astype(F32), sw64)
    f2a = jnp.where(first, p, 0.0)
    f2b = jnp.broadcast_to((lane == 1).astype(F32), p.shape)
    ref.f1[quarter] = jnp.concatenate([f1a, f1b], axis=1).astype(BF16)
    ref.f2[quarter] = jnp.concatenate([f2a, f2b], axis=1).astype(BF16)
    ref.colt[quarter] = p.T


def pair_weights(ref, town, row, col, zh):
    zl, y = col // 16, lax.rem(col // 2, 8)
    lane = lanes()
    k12 = ((lane // 2).astype(F32) < town).astype(F32)
    half = (row // 2).astype(F32)
    ln2 = 0.6931471805599453
    hi = float(ml_dtypes.bfloat16(ln2))
    mid = float(ml_dtypes.bfloat16(ln2 - hi))
    lo = ln2 - hi - mid
    ref.table[...] = jnp.zeros_like(ref.table)
    for t, offset in enumerate(OFFSETS):
        for core in range(2):
            g = 2 * t + core
            if offset[2]:
                weight = k12
            else:
                chip = chip_at(zl, y, offset, 1)
                k21 = (half < ref.t2[2 * chip + core]).astype(F32)
                weight = k12 + k21
            two = weight > 1.5
            ref.table[10 + g:11 + g, :] = jnp.where(weight < 0.5, BIG, jnp.where(two, hi, 0.0))
            ref.table[10 + RG + g:11 + RG + g, :] = jnp.where(two, mid, 0.0)
            ref.table[10 + 2 * RG + g:11 + 2 * RG + g, :] = jnp.where(two, lo, 0.0)
    table = ref.table[...].astype(BF16)

    def body(quarter, carry):
        x = lax.broadcasted_iota(jnp.int32, (QCOLS, 128), 0) // M
        zq = lax.rem(zh + quarter + 1, 4)
        hot = (lax.broadcasted_iota(jnp.int32, (QCOLS, 128), 1) == zq * 4 + x).astype(F32).astype(BF16)
        logs = dot_nt(hot, table).astype(BF16)
        ref.b_op[quarter, 0:QCOLS, 128:256] = ref.b_op[quarter, 0:QCOLS, 128:256] + logs
        return carry

    lax.fori_loop(0, QUART, body, 0)


def pair_step(ref, step, quarter):
    a = ref.a_op[pl.ds(step * RROWS, RROWS), :]
    es = dot_nt(a, ref.b_op[quarter])
    kept = jnp.exp(es[:, :QCOLS])
    coef = kept * es[:, QCOLS:]
    kb, cb = kept.astype(BF16), coef.astype(BF16)
    ref.racc[pl.ds(step * RROWS, RROWS), :] += dot(kb, ref.f1[quarter]) + dot(cb, ref.f2[quarter])
    ref.c1[quarter] += dot(ref.f1t[step], kb)
    ref.c2[quarter] += dot(ref.f2t[step], cb)


def finish_rows(ref, step):
    acc = ref.racc[pl.ds(step * RROWS, RROWS), :]
    low, high = acc[:, :128], acc[:, 128:]
    ks, cs = high[:, 0:1], high[:, 1:2]
    p = ref.rowbuf[pl.ds(step * RS_GROUPS, RS_GROUPS)].reshape(RROWS, 128).astype(F32)
    sw = pltpu.roll(p, 64, 1)
    grad = low + jnp.where(lanes() < 64, p * (-cs), high) + sw * (ks * (1.0 / 64))
    grad = grad.reshape(RS_GROUPS, M, 128)
    ref.rsend[pl.ds(step * RS_GROUPS, RS_GROUPS)] = grad.astype(BF16)
    ref.rowg[...] = grad
    ref.lossv[...] += jnp.sum(high, axis=0, keepdims=True)


def finish_cols(ref, quarter):
    g1, g2 = ref.c1[quarter], ref.c2[quarter]
    pt = ref.colt[quarter]
    xt, st = pt[0:64], pt[64:128]
    ks = g1[192:193] * (1.0 / 64)
    cs = g2[64:65]
    gx = g2[0:64] + g1[0:64] - xt * cs + st * ks
    gs = g1[64:128] + g1[128:192] + xt * ks
    grad = jnp.concatenate([gx, gs], axis=0).T.reshape(4, M, 128)
    ref.csend[pl.ds(quarter * 4, 4)] = grad.astype(BF16)
    ref.colg[...] = grad


def chip_at(zl, y, offset, sign):
    other, dy, _ = offset
    z = lax.rem(zl + other, 2)
    if dy is None:
        from_z = zl if sign > 0 else z
        dy = 4 * from_z
    return z * 8 + lax.rem(y + sign * dy + 16, 8)


class Refs:
    def __init__(self, names, refs):
        for name, r in zip(names, refs):
            setattr(self, name, r)


SCRATCH = dict(
    own=pltpu.VMEM((M, 128), BF16),
    rowbuf=pltpu.VMEM((RG, M, 128), BF16),
    colbuf=pltpu.VMEM((NROW, M, 128), BF16),
    t1=pltpu.VMEM((NROW, 1, 128), F32),
    t2=pltpu.VMEM((NCOL, 1, 128), F32),
    tsrc=pltpu.VMEM((1, 128), F32),
    tvec=pltpu.VMEM((1, 128), F32),
    table=pltpu.VMEM((128, 128), F32),
    a_op=pltpu.VMEM((RG * M, 256), BF16),
    b_op=pltpu.VMEM((QUART, 2 * QCOLS, 256), BF16),
    f1=pltpu.VMEM((QUART, QCOLS, 256), BF16),
    f2=pltpu.VMEM((QUART, QCOLS, 256), BF16),
    f1t=pltpu.VMEM((SUPER, 208, RROWS), BF16),
    f2t=pltpu.VMEM((SUPER, 80, RROWS), BF16),
    colt=pltpu.VMEM((QUART, 128, QCOLS), F32),
    racc=pltpu.VMEM((RG * M, 256), F32),
    c1=pltpu.VMEM((QUART, 208, QCOLS), F32),
    c2=pltpu.VMEM((QUART, 80, QCOLS), F32),
    rsend=pltpu.VMEM((RG, M, 128), BF16),
    csend=pltpu.VMEM((NROW, M, 128), BF16),
    rowg=pltpu.VMEM((RS_GROUPS, M, 128), F32),
    colg=pltpu.VMEM((4, M, 128), F32),
    rrow=pltpu.VMEM((RG, M, 128), BF16),
    rcol=pltpu.VMEM((NROW, M, 128), BF16),
    lossv=pltpu.VMEM((1, 128), F32),
    lsum=pltpu.VMEM((1, 128), F32),
    la=pltpu.VMEM((NCOL, 1, 128), F32),
    lb=pltpu.VMEM((NROW, 1, 128), F32),
)
SEMS = dict(
    t1=NROW, t2=NCOL, col=NROW, row=RG, rr=RG, rc=NROW, la=NCOL, lb=NROW,
)


def kernel(samples, scores, groups, out_x, out_s, out_loss, *rest):
    ref = Refs(SCRATCH, rest[:len(SCRATCH)])
    sems = rest[len(SCRATCH):]
    send = Refs(SEMS, sems[:len(SEMS)])
    recv = Refs(SEMS, sems[len(SEMS):])
    row, col = lax.axis_index("row"), lax.axis_index("col")
    zh, x = row // 4, lax.rem(row, 4)
    zl, y, core = col // 16, lax.rem(col // 2, 8), lax.rem(col, 2)
    sib = col + 1 - 2 * core

    barrier = pltpu.get_barrier_semaphore()

    def greet_col(d, carry):
        pl.semaphore_signal(barrier, inc=1, device_id=(lax.rem(row + d, NROW), col), device_id_type=MESH)
        return carry

    def greet_row(d, carry):
        pl.semaphore_signal(barrier, inc=1, device_id=(row, lax.rem(col + d, NCOL)), device_id_type=MESH)
        return carry

    lax.fori_loop(1, NROW, greet_col, 0)
    lax.fori_loop(1, NCOL, greet_row, 0)

    own = jnp.concatenate([samples[...], scores[...]], axis=1)
    ref.own[...] = own
    ref.rowbuf[2 * (CHUNKS - 1) + core] = own
    ref.colbuf[12 + x] = own
    town = groups[0, 0].astype(F32)
    tfull = jnp.full((1, 128), town, F32)
    ref.tsrc[...] = tfull
    ref.t1[row] = tfull
    ref.racc[...] = jnp.zeros_like(ref.racc)
    ref.c1[...] = jnp.zeros_like(ref.c1)
    ref.c2[...] = jnp.zeros_like(ref.c2)
    ref.lossv[...] = jnp.zeros_like(ref.lossv)

    pl.semaphore_wait(barrier, NROW + NCOL - 2)

    def copy(src, dst, ssem, rsem, to_row, to_col):
        return pltpu.make_async_remote_copy(
            src_ref=src, dst_ref=dst, send_sem=ssem, recv_sem=rsem,
            device_id=(to_row, to_col), device_id_type=MESH,
        )

    def t1_copy(d):
        return copy(ref.tsrc, ref.t1.at[row], send.t1.at[d], recv.t1.at[row], lax.rem(row + d, NROW), col)

    def t2_copy(d):
        return copy(ref.tvec, ref.t2.at[col], send.t2.at[d], recv.t2.at[col], row, lax.rem(col + d, NCOL))

    def z_copy(d):
        slot = (3 - d) * 4 + x
        return copy(ref.own, ref.colbuf.at[slot], send.col.at[d], recv.col.at[slot],
                    lax.rem(zh + d, 4) * 4 + x, col)

    def x_copy(quarter, d):
        slot = quarter * 4 + x
        src = ref.own if quarter == 3 else ref.colbuf.at[slot]
        return copy(src, ref.colbuf.at[slot], send.col.at[4 + 3 * quarter + d - 1], recv.col.at[slot],
                    zh * 4 + lax.rem(x + d, 4), col)

    def row_copy(t):
        chip = chip_at(zl, y, OFFSETS[t], -1)
        slot = 2 * t + core
        return copy(ref.own, ref.rowbuf.at[slot], send.row.at[t], recv.row.at[slot], row, 2 * chip + core)

    def sib_copy(t):
        slot = 2 * t + core
        src = ref.own if t == CHUNKS - 1 else ref.rowbuf.at[slot]
        return copy(src, ref.rowbuf.at[slot], send.row.at[CHUNKS - 1 + t], recv.row.at[slot], row, sib)

    def rr_copy(t, b):
        if t == CHUNKS - 1:
            return copy(ref.rsend.at[2 * t + 1 - core], ref.rrow.at[2 * t + core], send.rr.at[2 * t],
                        recv.rr.at[2 * t + core], row, sib)
        chip = chip_at(zl, y, OFFSETS[t], 1)
        slot = 2 * t + core
        return copy(ref.rsend.at[2 * t + b], ref.rrow.at[slot], send.rr.at[2 * t + b], recv.rr.at[slot],
                    row, 2 * chip + b)

    def rc_copy(quarter, k):
        if quarter == 3:
            xs = lax.rem(x + k, 4)
            to = zh * 4 + xs
            sem = 12 + k
        else:
            xs = k
            to = lax.rem(zh + quarter + 1, 4) * 4 + xs
            sem = quarter * 4 + k
        there = lax.rem(row - to + NROW, NROW)
        return copy(ref.csend.at[quarter * 4 + xs], ref.rcol.at[there], send.rc.at[sem], recv.rc.at[there], to, col)

    def la_copy(d):
        return copy(ref.lossv, ref.la.at[col], send.la.at[d], recv.la.at[col], row, lax.rem(col + d, NCOL))

    def lb_copy(d):
        return copy(ref.lsum, ref.lb.at[row], send.lb.at[d], recv.lb.at[row], lax.rem(row + d, NROW), col)

    def each(start, stop, act):
        def body(d, carry):
            act(d)
            return carry
        lax.fori_loop(start, stop, body, 0)

    def landed(buf, sem, slot):
        copy(buf.at[slot], buf.at[slot], sem.at[slot], sem.at[slot], row, sib).wait_recv()

    for d in range(1, 4):
        z_copy(d).start()
    each(1, NROW, lambda d: t1_copy(d).start())
    for t in range(CHUNKS - 1):
        row_copy(t).start()
    for d in range(1, 4):
        x_copy(3, d).start()
    sib_copy(CHUNKS - 1).start()

    for quarter in range(3):
        landed(ref.colbuf, recv.col, quarter * 4 + x)
        for d in range(1, 4):
            x_copy(quarter, d).start()

    each(1, NROW, lambda d: landed(ref.t1, recv.t1, lax.rem(row + d, NROW)))
    lane3 = lax.broadcasted_iota(jnp.int32, (NROW, 1, 128), 2)
    slot3 = lax.broadcasted_iota(jnp.int32, (NROW, 1, 128), 0)
    tvec = jnp.sum(jnp.where(lane3 == slot3, ref.t1[...], 0.0), axis=0)
    ref.tvec[...] = tvec
    ref.t2[col] = tvec
    each(1, NCOL, lambda d: t2_copy(d).start())

    for t in range(CHUNKS - 1):
        landed(ref.rowbuf, recv.row, 2 * t + core)
        sib_copy(t).start()

    each(1, 4, lambda d: landed(ref.colbuf, recv.col, 12 + lax.rem(x + d, 4)))
    for quarter in range(3):
        for d in range(1, 4):
            landed(ref.colbuf, recv.col, quarter * 4 + lax.rem(x + d, 4))
    each(0, QUART, lambda quarter: prep_cols(ref, quarter))
    each(0, CHUNKS, lambda t: landed(ref.rowbuf, recv.row, 2 * t + 1 - core))
    each(0, SUPER, lambda step: prep_rows(ref, step))
    each(1, NCOL, lambda d: landed(ref.t2, recv.t2, lax.rem(col + d, NCOL)))
    pair_weights(ref, town, row, col, zh)

    for quarter in range(3):
        each(0, SUPER, lambda step: pair_step(ref, step, quarter))
        finish_cols(ref, quarter)
        for k in range(4):
            rc_copy(quarter, k).start()
    for step in range(SUPER):
        pair_step(ref, step, 3)
        finish_rows(ref, step)
        for t in range(3 * step, 3 * step + 3):
            for b in range(1 if t == CHUNKS - 1 else 2):
                rr_copy(t, b).start()

    lane = lanes()
    own32 = ref.own[...].astype(F32)
    kept_diag = ((row // 2).astype(F32) < jnp.full((1, 128), town, F32)).astype(F32)
    loss_lanes = jnp.where(lane == 0, -1.0 / 32, jnp.where(lane == 1, 64.0, 0.0))
    s2 = jnp.sum(jnp.where(lane < 64, 1.0 / 64, own32 * own32 * (1.0)), axis=0, keepdims=True)
    ref.lossv[...] = ref.lossv[...] * loss_lanes - kept_diag * s2
    ref.la[col] = ref.lossv[...]
    each(1, NCOL, lambda d: la_copy(d).start())

    finish_cols(ref, 3)
    for k in range(1, 4):
        rc_copy(3, k).start()

    t2 = ref.t2[...]
    lane_n = lax.broadcasted_iota(jnp.int32, (NCOL, 1, 128), 2)
    diag = ((lane_n // 2).astype(F32) < t2).astype(F32)
    pairs = jnp.sum(jnp.sum(t2 * (128.0 * 2048.0) - 64.0 * diag, axis=0), axis=1, keepdims=True)
    scale = EVERYONE / pairs

    each(1, NCOL, lambda d: landed(ref.la, recv.la, lax.rem(col + d, NCOL)))
    lsum = jnp.sum(ref.la[...], axis=0)
    ref.lsum[...] = lsum
    ref.lb[row] = lsum
    each(1, NROW, lambda d: lb_copy(d).start())

    total = ref.rowg[2 * (CHUNKS - 1) - RS_GROUPS * (SUPER - 1) + core] + ref.colg[x]
    total = total - jnp.where(lane < 64, 0.0, 2.0 * kept_diag * own32)
    each(0, CHUNKS - 1, lambda t: (landed(ref.rrow, recv.rr, 2 * t), landed(ref.rrow, recv.rr, 2 * t + 1)))
    landed(ref.rrow, recv.rr, 2 * (CHUNKS - 1) + 1 - core)
    total = total + jnp.sum(ref.rrow[0:RG - 2].astype(F32), axis=0)
    total = total + ref.rrow[2 * (CHUNKS - 1) + 1 - core].astype(F32)
    each(1, NROW, lambda d: landed(ref.rcol, recv.rc, d))
    total = total + jnp.sum(ref.rcol[1:NROW].astype(F32), axis=0)
    total = total * scale
    out_x[...] = total[:, :64]
    out_s[...] = total[:, 64:]

    each(1, NROW, lambda d: landed(ref.lb, recv.lb, lax.rem(row + d, NROW)))
    out_loss[...] = jnp.sum(jnp.sum(ref.lb[...], axis=0), axis=1, keepdims=True) / pairs

    for d in range(1, 4):
        z_copy(d).wait_send()
    for quarter in range(QUART):
        for d in range(1, 4):
            x_copy(quarter, d).wait_send()
    for t in range(CHUNKS - 1):
        row_copy(t).wait_send()
    for t in range(CHUNKS):
        sib_copy(t).wait_send()
    for t in range(CHUNKS):
        for b in range(1 if t == CHUNKS - 1 else 2):
            rr_copy(t, b).wait_send()
    for quarter in range(QUART):
        for k in range(1 if quarter == 3 else 0, 4):
            rc_copy(quarter, k).wait_send()
    each(1, NROW, lambda d: t1_copy(d).wait_send())
    each(1, NCOL, lambda d: t2_copy(d).wait_send())
    each(1, NCOL, lambda d: la_copy(d).wait_send())
    each(1, NROW, lambda d: lb_copy(d).wait_send())


def shards(samples, scores, tile_groups):
    vmem = pl.BlockSpec(memory_space=pltpu.VMEM)
    out_x, out_s, loss = pl.pallas_call(
        kernel,
        out_shape=(
            jax.ShapeDtypeStruct((M, 64), F32),
            jax.ShapeDtypeStruct((M, 64), F32),
            jax.ShapeDtypeStruct((1, 1), F32),
        ),
        in_specs=[vmem, vmem, pl.BlockSpec(memory_space=pltpu.SMEM)],
        out_specs=(vmem, vmem, vmem),
        scratch_shapes=list(SCRATCH.values())
        + [pltpu.SemaphoreType.DMA((n,)) for n in SEMS.values()] * 2,
        compiler_params=pltpu.CompilerParams(
            collective_id=0, has_side_effects=True, vmem_limit_bytes=40 * 2**20
        ),
    )(samples, scores, tile_groups)
    return out_x, out_s, loss[0, 0]


def solution(mesh):
    placed = (P(("row", "col"), None), P(("row", "col"), None), P("row", "col"))
    return jax.shard_map(
        shards,
        mesh=mesh,
        in_specs=placed,
        out_specs=(P(("row", "col"), None), P(("row", "col"), None), P()),
        check_vma=False,
    )
```

```python
import jax
import jax.numpy as jnp
from jax import lax
from jax.experimental import pallas as pl
from jax.experimental.pallas import tpu as pltpu
from jax.sharding import PartitionSpec as P

MESH = pl.DeviceIdType.MESH
F32 = jnp.float32
BF16 = jnp.bfloat16

NROW, NCOL = 16, 32
M = 64
CHUNKS = 9
RG = 2 * CHUNKS
SUPER = 3
GROUPS = RG // SUPER
ROWS = GROUPS * M
QUART = 4
QCOLS = 4 * M
EVERYONE = float(M * NROW * NCOL)
NSLOT = 14

OFFSETS = (
    (0, 4, True), (0, 3, False), (1, -3, False),
    (1, None, False), (1, 2, False), (0, -2, False),
    (0, 1, False), (1, -1, False), (0, 0, True),
)


def split3(value):
    hi = value.astype(BF16).astype(F32)
    rest = value - hi
    mid = rest.astype(BF16).astype(F32)
    return hi, mid, rest - mid


def dot(a, b):
    return lax.dot_general(a, b, (((1,), (0,)), ((), ())), preferred_element_type=F32)


def dot_nt(a, b):
    return lax.dot_general(a, b, (((1,), (1,)), ((), ())), preferred_element_type=F32)


def lanes(rows=1, width=128):
    return lax.broadcasted_iota(jnp.int32, (rows, width), 1)


def squares(p, sw):
    q = p * jnp.where(lanes() < 64, p, sw)
    hi = q.astype(BF16)
    return jnp.concatenate([hi, (q - hi.astype(F32)).astype(BF16)], axis=1)


def sum_weights(e_lanes, s_lanes):
    k = lax.broadcasted_iota(jnp.int32, (256, 128), 0) % 128
    lane = lax.broadcasted_iota(jnp.int32, (256, 128), 1)
    is_x = k < 64
    out = jnp.zeros((256, 128), F32)
    if e_lanes is not None:
        in_e = (lane >= e_lanes) & (lane < e_lanes + 3)
        out = jnp.where(in_e & is_x, -(2.0 ** -7), out)
    if s_lanes is not None:
        in_s = (lane >= s_lanes) & (lane < s_lanes + 3)
        out = jnp.where(in_s, jnp.where(is_x, -(2.0 ** -18), 2.0 ** -12), out)
    return out.astype(BF16)


def pick3(value):
    hi, mid, lo = split3(value)
    part = lanes() % 3
    return jnp.where(part == 0, hi, jnp.where(part == 1, mid, lo))


def prep_rows(ref, step):
    pair = ref.rowbuf[pl.ds(step * GROUPS, GROUPS)].reshape(ROWS, 128)
    p = pair.astype(F32)
    sw = pltpu.roll(p, 64, 1)
    lane = lanes()
    sums = dot(squares(p, sw), sum_weights(0, 6))
    one = (((lane >= 3) & (lane < 6)) | (lane == 9)).astype(F32)
    misc = pick3(sums) + one
    ext = jnp.where(lane < 64, misc, p).astype(BF16)
    ref.a_op[step] = jnp.concatenate([pair, ext], axis=1)
    pt = p.T
    xt, st = pt[0:64], pt[64:128]
    ones = jnp.ones((16, ROWS), F32)
    at = pl.ds(step * ROWS, ROWS)
    ref.f1t[:, at] = jnp.concatenate([st * (-1.0 / 64), st, xt * (-1.0 / 64), ones], axis=0).astype(BF16)
    ref.f2t[:, at] = jnp.concatenate([xt, ones], axis=0).astype(BF16)


def prep_cols(ref, quarter):
    pair = ref.colbuf[pl.ds(quarter * 4, 4)].reshape(QCOLS, 128)
    p = pair.astype(F32)
    sw = pltpu.roll(p, 64, 1)
    lane = lanes()
    first = lane < 64
    sq = squares(p, sw)
    sums_e = dot(sq, sum_weights(3, None))
    sums_s = dot(sq, sum_weights(None, 3))
    u = p * jnp.where(first, 2.0 ** -17, 2.0 ** -6) - sw * (2.0 ** -12)
    u_hi = u.astype(BF16)
    e1 = jnp.where(first, p * (1.0 / 64), 0.0).astype(BF16)
    e2 = pick3(sums_e) + (lane < 3).astype(F32)
    s2 = pick3(sums_s) + ((lane >= 6) & (lane < 9)).astype(F32) + jnp.where(lane == 9, 33.0 / 2048, 0.0)
    s2 = jnp.where(first, s2, u - u_hi.astype(F32))
    ref.b_op[quarter, 0:QCOLS, :] = jnp.concatenate([e1, e2.astype(BF16)], axis=1)
    ref.b_op[quarter, QCOLS:2 * QCOLS, :] = jnp.concatenate([u_hi, s2.astype(BF16)], axis=1)
    sw64 = sw * (-1.0 / 64)
    f1a = jnp.where(first, sw64, p)
    f1b = jnp.where(first, (lane == 0).astype(F32), sw64)
    f2a = jnp.where(first, p, 0.0)
    f2b = jnp.broadcast_to((lane == 1).astype(F32), p.shape)
    at = pl.ds(quarter * QCOLS, QCOLS)
    ref.f1[at, :] = jnp.concatenate([f1a, f1b], axis=1).astype(BF16)
    ref.f2[at, :] = jnp.concatenate([f2a, f2b], axis=1).astype(BF16)
    ref.colt[quarter] = p.T


def pair_step(ref, step, quarter):
    es = dot_nt(ref.a_op[step], ref.b_op[quarter])
    kept = jnp.exp(es[:, :QCOLS])
    coef = kept * es[:, QCOLS:]
    at = (pl.ds(step * ROWS, ROWS), slice(quarter * QCOLS, (quarter + 1) * QCOLS))
    ref.kmat[at] = kept.astype(BF16)
    ref.cmat[at] = coef.astype(BF16)
    to = (step, slice(0, GROUPS), slice(quarter * QCOLS, (quarter + 1) * QCOLS))
    ref.usum[to] = jnp.sum((coef * 64.0 - kept * (1.0 / 32)).reshape(GROUPS, M, QCOLS), axis=1)


def expansion(ref, row, zh, x):
    lane = lanes(1, NROW * M)
    slot = lane // M
    quarter, dx = slot // 4, slot % 4
    other = ((zh + quarter + 1) % 4) * 4 + (x + dx) % 4
    place = (other - row + NROW) % NROW
    hot = (lax.broadcasted_iota(jnp.int32, (NROW, NROW * M), 0) == place).astype(F32)
    ref.spread[...] = jnp.concatenate([hot, jnp.zeros((128 - NROW, NROW * M), F32)], axis=0).astype(BF16)


def pair_weights(ref, town, row):
    lane = lanes()
    theirs = ((row + lane) % NROW) // 2
    k12 = (theirs.astype(F32) < town).astype(F32)
    half = (row // 2).astype(F32)
    ref.table[...] = jnp.zeros_like(ref.table)
    for step in range(SUPER):
        for i in range(GROUPS):
            rel, t = i // 3, 3 * step + i % 3
            weight = k12
            if not OFFSETS[t][2]:
                weight = k12 + (half < ref.t2[2 * (t - 1) + rel]).astype(F32)
            ref.table[8 * step + i:8 * step + i + 1, :] = weight
    ref.wtab[...] = dot(ref.table[...].astype(BF16), ref.spread[...]).reshape(4, 8, NROW * M)


def weighted(mat, ref, step, start, width):
    at = slice(start, start + width)
    out = []
    for i in range(GROUPS):
        w = jnp.broadcast_to(ref.wtab[step, i:i + 1, at], (16, width)).astype(BF16)
        part = mat[step * ROWS + i * M:step * ROWS + (i + 1) * M, at]
        out.append(part * jnp.concatenate([w] * (M // 16), axis=0))
    return jnp.concatenate(out, axis=0)


def row_results(ref, step):
    kb = weighted(ref.kmat, ref, step, 0, NROW * M)
    cb = weighted(ref.cmat, ref, step, 0, NROW * M)
    acc = dot(kb, ref.f1[...]) + dot(cb, ref.f2[...])
    low, high = acc[:, :128], acc[:, 128:]
    ks, cs = high[:, 0:1], high[:, 1:2]
    p = ref.rowbuf[step * GROUPS:(step + 1) * GROUPS].reshape(ROWS, 128).astype(F32)
    sw = pltpu.roll(p, 64, 1)
    grad = low + jnp.where(lanes() < 64, p * (-cs), high) + sw * (ks * (1.0 / 64))
    grad = grad.reshape(GROUPS, M, 128)
    ref.rowg[step] = grad[0:3]
    ref.sibsend[step] = grad[3:6].astype(BF16)


def col_results(ref, quarter):
    kb = jnp.concatenate([weighted(ref.kmat, ref, s, quarter * QCOLS, QCOLS) for s in range(SUPER)], axis=0)
    cb = jnp.concatenate([weighted(ref.cmat, ref, s, quarter * QCOLS, QCOLS) for s in range(SUPER)], axis=0)
    g1 = dot(ref.f1t[...], kb)
    g2 = dot(ref.f2t[...], cb)
    pt = ref.colt[quarter]
    xt, st = pt[0:64], pt[64:128]
    ks = g1[192:193] * (1.0 / 64)
    cs = g2[64:65]
    gx = g2[0:64] + g1[0:64] - xt * cs + st * ks
    gs = g1[64:128] + g1[128:192] + xt * ks
    grad = jnp.concatenate([gx, gs], axis=0).T.reshape(4, M, 128)
    ref.csend[quarter * 4:quarter * 4 + 4] = grad.astype(BF16)
    if quarter == 3:
        ref.colown[...] = grad[0]


def chip_at(zl, y, offset, sign):
    other, dy, _ = offset
    z = lax.rem(zl + other, 2)
    if dy is None:
        from_z = zl if sign > 0 else z
        dy = 4 * from_z
    return z * 8 + lax.rem(y + sign * dy + 16, 8)


class Refs:
    def __init__(self, names, refs):
        for name, r in zip(names, refs):
            setattr(self, name, r)


SCRATCH = dict(
    xin=pltpu.VMEM((M, 64), BF16),
    sin=pltpu.VMEM((M, 64), BF16),
    own=pltpu.VMEM((M, 128), BF16),
    rowbuf=pltpu.VMEM((RG, M, 128), BF16),
    colbuf=pltpu.VMEM((NROW, M, 128), BF16),
    t1=pltpu.VMEM((NROW, 1, 128), F32),
    t2=pltpu.VMEM((NSLOT, 1, 128), F32),
    tsrc=pltpu.VMEM((1, 128), F32),
    tvec=pltpu.VMEM((1, 128), F32),
    table=pltpu.VMEM((32, 128), F32),
    spread=pltpu.VMEM((128, NROW * M), BF16),
    wtab=pltpu.VMEM((4, 8, NROW * M), F32),
    a_op=pltpu.VMEM((SUPER, ROWS, 256), BF16),
    b_op=pltpu.VMEM((QUART, 2 * QCOLS, 256), BF16),
    f1=pltpu.VMEM((NROW * M, 256), BF16),
    f2=pltpu.VMEM((NROW * M, 256), BF16),
    f1t=pltpu.VMEM((208, RG * M), BF16),
    f2t=pltpu.VMEM((80, RG * M), BF16),
    colt=pltpu.VMEM((QUART, 128, QCOLS), F32),
    kmat=pltpu.VMEM((RG * M, NROW * M), BF16),
    cmat=pltpu.VMEM((RG * M, NROW * M), BF16),
    usum=pltpu.VMEM((SUPER, 8, NROW * M), F32),
    rowg=pltpu.VMEM((SUPER, 3, M, 128), F32),
    sibsend=pltpu.VMEM((SUPER, 3, M, 128), BF16),
    sibrecv=pltpu.VMEM((SUPER, 3, M, 128), BF16),
    rsend=pltpu.VMEM((CHUNKS - 1, M, 128), BF16),
    csend=pltpu.VMEM((NROW, M, 128), BF16),
    rowown=pltpu.VMEM((M, 128), F32),
    colown=pltpu.VMEM((M, 128), F32),
    rrow=pltpu.VMEM((CHUNKS - 1, M, 128), BF16),
    rcol=pltpu.VMEM((NROW - 1, M, 128), BF16),
    lossv=pltpu.VMEM((1, 128), F32),
    lsum=pltpu.VMEM((1, 128), F32),
    la=pltpu.VMEM((NCOL, 1, 128), F32),
    lb=pltpu.VMEM((NROW, 1, 128), F32),
)
SEND = dict(load=2, t1=1, t2=1, col=1, row=1, sib=1, sg=1, rr=1, rc=1, la=1, lb=1)
RECV = dict(t1=1, t2=1, col=QUART, row=SUPER, sib=SUPER, sg=SUPER, rr=1, rc=1, la=1, lb=1)


def kernel(samples, scores, groups, out_x, out_s, out_loss, *rest):
    ref = Refs(SCRATCH, rest[:len(SCRATCH)])
    sems = rest[len(SCRATCH):]
    send = Refs(SEND, sems[:len(SEND)])
    recv = Refs(RECV, sems[len(SEND):])
    row, col = lax.axis_index("row"), lax.axis_index("col")
    zh, x = row // 4, lax.rem(row, 4)
    zl, y, core = col // 16, lax.rem(col // 2, 8), lax.rem(col, 2)
    sib = col + 1 - 2 * core

    def each(start, stop, act):
        def body(d, carry):
            act(d)
            return carry
        lax.fori_loop(start, stop, body, 0)

    barrier = pltpu.get_barrier_semaphore()

    def greet(to_row, to_col):
        pl.semaphore_signal(barrier, inc=1, device_id=(to_row, to_col), device_id_type=MESH)

    each(1, NROW, lambda d: greet(lax.rem(row + d, NROW), col))
    each(1, NCOL, lambda d: greet(row, lax.rem(col + d, NCOL)))

    loads = [pltpu.make_async_copy(samples, ref.xin, send.load.at[0]),
             pltpu.make_async_copy(scores, ref.sin, send.load.at[1])]
    for load in loads:
        load.start()
    town = groups[0, 0].astype(F32)
    tfull = jnp.full((1, 128), town, F32)
    ref.tsrc[...] = tfull
    ref.t1[0] = tfull
    expansion(ref, row, zh, x)
    for load in loads:
        load.wait()
    own = jnp.concatenate([ref.xin[...], ref.sin[...]], axis=1)
    ref.own[...] = own
    ref.rowbuf[RG - 4] = own
    ref.colbuf[12] = own
    pl.semaphore_wait(barrier, NROW + NCOL - 2)

    def copy(src, dst, ssem, rsem, to_row, to_col):
        return pltpu.make_async_remote_copy(
            src_ref=src, dst_ref=dst, send_sem=ssem, recv_sem=rsem,
            device_id=(to_row, to_col), device_id_type=MESH,
        )

    def t1_copy(d):
        return copy(ref.tsrc, ref.t1.at[NROW - d], send.t1.at[0], recv.t1.at[0], lax.rem(row + d, NROW), col)

    def t2_copy(t, b):
        chip = chip_at(zl, y, OFFSETS[t], -1)
        slot = 2 * (t - 1) + lax.rem(core + b, 2)
        return copy(ref.tvec, ref.t2.at[slot], send.t2.at[0], recv.t2.at[0], row, 2 * chip + b)

    def col_copy(quarter, dx):
        dz = (quarter + 1) % 4
        to = lax.rem(zh + 4 - dz, 4) * 4 + lax.rem(x + 4 - dx, 4)
        return copy(ref.own, ref.colbuf.at[quarter * 4 + dx], send.col.at[0], recv.col.at[quarter], to, col)

    def row_copy(t):
        chip = chip_at(zl, y, OFFSETS[t], -1)
        slot = GROUPS * (t // 3) + t % 3
        return copy(ref.own, ref.rowbuf.at[slot], send.row.at[0], recv.row.at[t // 3], row, 2 * chip + core)

    def sib_copy(step):
        at = GROUPS * step
        return copy(ref.rowbuf.at[at:at + 3], ref.rowbuf.at[at + 3:at + 6], send.sib.at[0], recv.sib.at[step], row, sib)

    def sg_copy(step):
        return copy(ref.sibsend.at[step], ref.sibrecv.at[step], send.sg.at[0], recv.sg.at[step], row, sib)

    def rr_copy(t):
        chip = chip_at(zl, y, OFFSETS[t], 1)
        return copy(ref.rsend.at[t], ref.rrow.at[t], send.rr.at[0], recv.rr.at[0], row, 2 * chip + core)

    def rc_copy(quarter, dx):
        dz = (quarter + 1) % 4
        to = lax.rem(zh + dz, 4) * 4 + lax.rem(x + dx, 4)
        slot = quarter * 4 + dx - (1 if quarter == 3 else 0)
        return copy(ref.csend.at[quarter * 4 + dx], ref.rcol.at[slot], send.rc.at[0], recv.rc.at[0], to, col)

    def la_copy(d):
        return copy(ref.lossv, ref.la.at[NCOL - d], send.la.at[0], recv.la.at[0], row, lax.rem(col + d, NCOL))

    def lb_copy(d):
        return copy(ref.lsum, ref.lb.at[NROW - d], send.lb.at[0], recv.lb.at[0], lax.rem(row + d, NROW), col)

    def landed(buf, sem):
        copy(buf, buf, sem, sem, row, sib).wait_recv()

    def left(buf, sem):
        copy(buf, buf, sem, sem, row, sib).wait_send()

    each(1, NROW, lambda d: t1_copy(d).start())
    for t in range(CHUNKS - 1):
        row_copy(t).start()
    for quarter in (1, 0, 2, 3):
        for dx in (2, 1, 3, 0):
            if (quarter, dx) != (3, 0):
                col_copy(quarter, dx).start()

    def got_cols(quarter):
        at = quarter * 4
        landed(ref.colbuf.at[at + (1 if quarter == 3 else 0):at + 4], recv.col.at[quarter])
        prep_cols(ref, quarter)

    def got_rows(step):
        at = GROUPS * step
        landed(ref.rowbuf.at[at:at + (2 if step == 2 else 3)], recv.row.at[step])
        sib_copy(step).start()

    def got_sib(step):
        at = GROUPS * step
        landed(ref.rowbuf.at[at + 3:at + 6], recv.sib.at[step])
        prep_rows(ref, step)

    got_rows(2)
    got_cols(3)
    got_sib(2)
    pair_step(ref, 2, 3)
    got_cols(0)
    pair_step(ref, 2, 0)
    landed(ref.t1.at[1:NROW], recv.t1.at[0])
    lane3 = lax.broadcasted_iota(jnp.int32, (NROW, 1, 128), 2)
    slot3 = lax.broadcasted_iota(jnp.int32, (NROW, 1, 128), 0)
    ref.tvec[...] = jnp.sum(jnp.where(lane3 == slot3, ref.t1[...], 0.0), axis=0)
    for t in range(1, CHUNKS - 1):
        for b in range(2):
            t2_copy(t, b).start()
    got_rows(1)
    got_cols(2)
    got_rows(0)
    pair_step(ref, 2, 2)
    got_sib(1)
    pair_step(ref, 1, 3)
    pair_step(ref, 1, 0)
    pair_step(ref, 1, 2)
    got_cols(1)
    pair_step(ref, 2, 1)
    pair_step(ref, 1, 1)
    got_sib(0)
    for quarter in range(QUART):
        pair_step(ref, 0, quarter)
    landed(ref.t2, recv.t2.at[0])
    pair_weights(ref, town, row)

    lane = lanes()
    own32 = ref.own[...].astype(F32)
    kept_diag = jnp.where((row // 2).astype(F32) < jnp.full((1, 128), town, F32), 1.0, 0.0)
    part = jnp.zeros((1, NROW * M), F32)
    for step in range(SUPER):
        part = part + jnp.sum(ref.usum[step, 0:GROUPS] * ref.wtab[step, 0:GROUPS], axis=0, keepdims=True)
    s2 = jnp.sum(jnp.where(lane < 64, 1.0 / 64, own32 * own32), axis=0, keepdims=True)
    loss = jnp.sum(part, axis=1, keepdims=True) - jnp.sum(s2 * kept_diag, axis=1, keepdims=True)
    count = tfull * (128.0 * 2048.0) - 64.0 * kept_diag
    lossv = jnp.where(lane == 0, loss, jnp.where(lane == 1, count, 0.0))
    ref.lossv[...] = lossv
    ref.la[0] = lossv
    each(1, NCOL, lambda d: la_copy(d).start())

    def cols_out(quarter):
        col_results(ref, quarter)
        for dx in (2, 1, 3, 0):
            if (quarter, dx) != (3, 0):
                rc_copy(quarter, dx).start()

    def rows_out(step):
        row_results(ref, step)
        sg_copy(step).start()

    def rows_on(step):
        landed(ref.sibrecv.at[step], recv.sg.at[step])
        both = ref.rowg[step] + ref.sibrecv[step].astype(F32)
        if step == SUPER - 1:
            ref.rsend[6:8] = both[0:2].astype(BF16)
            ref.rowown[...] = both[2]
        else:
            ref.rsend[3 * step:3 * step + 3] = both.astype(BF16)
        for t in range(3 * step, min(3 * step + 3, CHUNKS - 1)):
            rr_copy(t).start()

    rows_out(0)
    cols_out(1)
    rows_on(0)
    rows_out(1)
    cols_out(0)
    rows_on(1)
    cols_out(2)
    rows_out(2)
    cols_out(3)
    rows_on(2)

    landed(ref.la.at[1:NCOL], recv.la.at[0])
    lsum = jnp.sum(ref.la[...], axis=0)
    ref.lsum[...] = lsum
    ref.lb[0] = lsum
    each(1, NROW, lambda d: lb_copy(d).start())

    total = ref.rowown[...] + ref.colown[...] - jnp.where(lane < 64, 0.0, 2.0 * kept_diag * own32)
    landed(ref.rrow, recv.rr.at[0])
    total = total + jnp.sum(ref.rrow[...].astype(F32), axis=0)
    landed(ref.rcol, recv.rc.at[0])
    total = total + jnp.sum(ref.rcol[...].astype(F32), axis=0)

    landed(ref.lb.at[1:NROW], recv.lb.at[0])
    sums = jnp.sum(ref.lb[...], axis=0)
    pairs = sums[:, 1:2]
    out_loss[...] = sums[:, 0:1] / pairs
    total = total * (EVERYONE / pairs)
    out_x[...] = total[:, :64]
    out_s[...] = total[:, 64:]

    left(ref.t1.at[1:NROW], send.t1.at[0])
    left(ref.t2, send.t2.at[0])
    left(ref.colbuf.at[1:NROW], send.col.at[0])
    left(ref.rrow, send.row.at[0])
    left(ref.rowbuf.at[0:CHUNKS], send.sib.at[0])
    left(ref.sibsend, send.sg.at[0])
    left(ref.rrow, send.rr.at[0])
    left(ref.rcol, send.rc.at[0])
    left(ref.la.at[1:NCOL], send.la.at[0])
    left(ref.lb.at[1:NROW], send.lb.at[0])


def shards(samples, scores, tile_groups):
    vmem = pl.BlockSpec(memory_space=pltpu.VMEM)
    hbm = pl.BlockSpec(memory_space=pl.ANY)
    out_x, out_s, loss = pl.pallas_call(
        kernel,
        out_shape=(
            jax.ShapeDtypeStruct((M, 64), F32),
            jax.ShapeDtypeStruct((M, 64), F32),
            jax.ShapeDtypeStruct((1, 1), F32),
        ),
        in_specs=[hbm, hbm, pl.BlockSpec(memory_space=pltpu.SMEM)],
        out_specs=(vmem, vmem, vmem),
        scratch_shapes=list(SCRATCH.values())
        + [pltpu.SemaphoreType.DMA((n,)) for n in (*SEND.values(), *RECV.values())],
        compiler_params=pltpu.CompilerParams(
            collective_id=0, has_side_effects=True, vmem_limit_bytes=48 * 2**20
        ),
    )(samples, scores, tile_groups)
    return out_x, out_s, loss[0, 0]


def solution(mesh):
    placed = (P(("row", "col"), None), P(("row", "col"), None), P("row", "col"))
    return jax.shard_map(
        shards,
        mesh=mesh,
        in_specs=placed,
        out_specs=(P(("row", "col"), None), P(("row", "col"), None), P()),
        check_vma=False,
    )
```

```python
import jax
import jax.numpy as jnp
from jax import lax
from jax.experimental import pallas as pl
from jax.experimental.pallas import tpu as pltpu
from jax.sharding import PartitionSpec as P

MESH = pl.DeviceIdType.MESH
F32 = jnp.float32
BF16 = jnp.bfloat16

NROW, NCOL = 16, 32
M = 64
CHUNKS = 9
RG = 2 * CHUNKS
SUPER = 3
GROUPS = RG // SUPER
ROWS = GROUPS * M
QUART = 4
QCOLS = 4 * M
EVERYONE = float(M * NROW * NCOL)
FAR_ROW = (10, 8, 9, 11, 6, 14, 4, 12, 5, 7, 13, 15, 2, 1, 3)
FAR_COL = tuple(sorted(range(1, 32), key=lambda d: -min((d // 2) % 8, 8 - (d // 2) % 8)))
NSLOT = 14

OFFSETS = (
    (0, 4, True), (0, 3, False), (1, -3, False),
    (1, None, False), (1, 2, False), (0, -2, False),
    (0, 1, False), (1, -1, False), (0, 0, True),
)


def split3(value):
    hi = value.astype(BF16).astype(F32)
    rest = value - hi
    mid = rest.astype(BF16).astype(F32)
    return hi, mid, rest - mid


def dot(a, b):
    return lax.dot_general(a, b, (((1,), (0,)), ((), ())), preferred_element_type=F32)


def dot_nt(a, b):
    return lax.dot_general(a, b, (((1,), (1,)), ((), ())), preferred_element_type=F32)


def lanes(rows=1, width=128):
    return lax.broadcasted_iota(jnp.int32, (rows, width), 1)


def squares(p, sw):
    q = p * jnp.where(lanes() < 64, p, sw)
    hi = q.astype(BF16)
    return jnp.concatenate([hi, (q - hi.astype(F32)).astype(BF16)], axis=1)


def sum_weights(e_lanes, s_lanes):
    k = lax.broadcasted_iota(jnp.int32, (256, 128), 0) % 128
    lane = lax.broadcasted_iota(jnp.int32, (256, 128), 1)
    is_x = k < 64
    out = jnp.zeros((256, 128), F32)
    if e_lanes is not None:
        in_e = (lane >= e_lanes) & (lane < e_lanes + 3)
        out = jnp.where(in_e & is_x, -(2.0 ** -7), out)
    if s_lanes is not None:
        in_s = (lane >= s_lanes) & (lane < s_lanes + 3)
        out = jnp.where(in_s, jnp.where(is_x, -(2.0 ** -18), 2.0 ** -12), out)
    return out.astype(BF16)


def pick3(value):
    hi, mid, lo = split3(value)
    part = lanes() % 3
    return jnp.where(part == 0, hi, jnp.where(part == 1, mid, lo))


def prep_rows(ref, step):
    pair = ref.rowbuf[pl.ds(step * GROUPS, GROUPS)].reshape(ROWS, 128)
    p = pair.astype(F32)
    sw = pltpu.roll(p, 64, 1)
    lane = lanes()
    sums = dot(squares(p, sw), sum_weights(0, 6))
    one = (((lane >= 3) & (lane < 6)) | (lane == 9)).astype(F32)
    misc = pick3(sums) + one
    ext = jnp.where(lane < 64, misc, p).astype(BF16)
    ref.a_op[step] = jnp.concatenate([pair, ext], axis=1)
    pt = p.T
    xt, st = pt[0:64], pt[64:128]
    ones = jnp.ones((16, ROWS), F32)
    at = pl.ds(step * ROWS, ROWS)
    ref.f1t[:, at] = jnp.concatenate([st * (-1.0 / 64), st, xt * (-1.0 / 64), ones], axis=0).astype(BF16)
    ref.f2t[:, at] = jnp.concatenate([xt, ones], axis=0).astype(BF16)


def prep_cols(ref, quarter):
    pair = ref.colbuf[pl.ds(quarter * 4, 4)].reshape(QCOLS, 128)
    p = pair.astype(F32)
    sw = pltpu.roll(p, 64, 1)
    lane = lanes()
    first = lane < 64
    sq = squares(p, sw)
    sums_e = dot(sq, sum_weights(3, None))
    sums_s = dot(sq, sum_weights(None, 3))
    u = p * jnp.where(first, 2.0 ** -17, 2.0 ** -6) - sw * (2.0 ** -12)
    u_hi = u.astype(BF16)
    e1 = jnp.where(first, p * (1.0 / 64), 0.0).astype(BF16)
    e2 = pick3(sums_e) + (lane < 3).astype(F32)
    s2 = pick3(sums_s) + ((lane >= 6) & (lane < 9)).astype(F32) + jnp.where(lane == 9, 33.0 / 2048, 0.0)
    s2 = jnp.where(first, s2, u - u_hi.astype(F32))
    ref.b_op[quarter, 0:QCOLS, :] = jnp.concatenate([e1, e2.astype(BF16)], axis=1)
    ref.b_op[quarter, QCOLS:2 * QCOLS, :] = jnp.concatenate([u_hi, s2.astype(BF16)], axis=1)
    sw64 = sw * (-1.0 / 64)
    f1a = jnp.where(first, sw64, p)
    f1b = jnp.where(first, (lane == 0).astype(F32), sw64)
    f2a = jnp.where(first, p, 0.0)
    f2b = jnp.broadcast_to((lane == 1).astype(F32), p.shape)
    at = pl.ds(quarter * QCOLS, QCOLS)
    ref.f1[at, :] = jnp.concatenate([f1a, f1b], axis=1).astype(BF16)
    ref.f2[at, :] = jnp.concatenate([f2a, f2b], axis=1).astype(BF16)
    ref.colt[quarter] = p.T


def pair_step(ref, step, quarter):
    es = dot_nt(ref.a_op[step], ref.b_op[quarter])
    kept = jnp.exp(es[:, :QCOLS])
    coef = kept * es[:, QCOLS:]
    at = (pl.ds(step * ROWS, ROWS), slice(quarter * QCOLS, (quarter + 1) * QCOLS))
    ref.kmat[at] = kept.astype(BF16)
    ref.cmat[at] = coef.astype(BF16)
    to = (step, slice(0, GROUPS), slice(quarter * QCOLS, (quarter + 1) * QCOLS))
    ref.usum[to] = jnp.sum((coef * 64.0 - kept * (1.0 / 32)).reshape(GROUPS, M, QCOLS), axis=1)


def expansion(ref, row, zh, x):
    lane = lanes(1, NROW * M)
    slot = lane // M
    quarter, dx = slot // 4, slot % 4
    other = ((zh + quarter + 1) % 4) * 4 + (x + dx) % 4
    place = (other - row + NROW) % NROW
    hot = (lax.broadcasted_iota(jnp.int32, (NROW, NROW * M), 0) == place).astype(F32)
    ref.spread[...] = jnp.concatenate([hot, jnp.zeros((128 - NROW, NROW * M), F32)], axis=0).astype(BF16)


def pair_weights(ref, town, row):
    lane = lanes()
    theirs = ((row + lane) % NROW) // 2
    k12 = (theirs.astype(F32) < town).astype(F32)
    half = (row // 2).astype(F32)
    ref.table[...] = jnp.zeros_like(ref.table)
    for step in range(SUPER):
        for i in range(GROUPS):
            rel, t = i // 3, 3 * step + i % 3
            weight = k12
            if not OFFSETS[t][2]:
                weight = k12 + (half < ref.t2[2 * (t - 1) + rel]).astype(F32)
            ref.table[8 * step + i:8 * step + i + 1, :] = weight
    ref.wtab[...] = dot(ref.table[...].astype(BF16), ref.spread[...]).reshape(4, 8, NROW * M)


def weighted(mat, ref, step, start, width):
    at = slice(start, start + width)
    out = []
    for i in range(GROUPS):
        w = jnp.broadcast_to(ref.wtab[step, i:i + 1, at], (16, width)).astype(BF16)
        part = mat[step * ROWS + i * M:step * ROWS + (i + 1) * M, at]
        out.append(part * jnp.concatenate([w] * (M // 16), axis=0))
    return jnp.concatenate(out, axis=0)


def row_results(ref, step):
    kb = weighted(ref.kmat, ref, step, 0, NROW * M)
    cb = weighted(ref.cmat, ref, step, 0, NROW * M)
    acc = dot(kb, ref.f1[...]) + dot(cb, ref.f2[...])
    low, high = acc[:, :128], acc[:, 128:]
    ks, cs = high[:, 0:1], high[:, 1:2]
    p = ref.rowbuf[step * GROUPS:(step + 1) * GROUPS].reshape(ROWS, 128).astype(F32)
    sw = pltpu.roll(p, 64, 1)
    grad = low + jnp.where(lanes() < 64, p * (-cs), high) + sw * (ks * (1.0 / 64))
    grad = grad.reshape(GROUPS, M, 128)
    ref.rowg[step] = grad[0:3]
    ref.sibsend[step] = grad[3:6].astype(BF16)


def col_results(ref, quarter):
    kb = jnp.concatenate([weighted(ref.kmat, ref, s, quarter * QCOLS, QCOLS) for s in range(SUPER)], axis=0)
    cb = jnp.concatenate([weighted(ref.cmat, ref, s, quarter * QCOLS, QCOLS) for s in range(SUPER)], axis=0)
    g1 = dot(ref.f1t[...], kb)
    g2 = dot(ref.f2t[...], cb)
    pt = ref.colt[quarter]
    xt, st = pt[0:64], pt[64:128]
    ks = g1[192:193] * (1.0 / 64)
    cs = g2[64:65]
    gx = g2[0:64] + g1[0:64] - xt * cs + st * ks
    gs = g1[64:128] + g1[128:192] + xt * ks
    grad = jnp.concatenate([gx, gs], axis=0).T.reshape(4, M, 128)
    ref.csend[quarter * 4:quarter * 4 + 4] = grad.astype(BF16)
    if quarter == 3:
        ref.colown[...] = grad[0]


def chip_at(zl, y, offset, sign):
    other, dy, _ = offset
    z = lax.rem(zl + other, 2)
    if dy is None:
        from_z = zl if sign > 0 else z
        dy = 4 * from_z
    return z * 8 + lax.rem(y + sign * dy + 16, 8)


class Refs:
    def __init__(self, names, refs):
        for name, r in zip(names, refs):
            setattr(self, name, r)


SCRATCH = dict(
    xin=pltpu.VMEM((M, 64), BF16),
    sin=pltpu.VMEM((M, 64), BF16),
    own=pltpu.VMEM((M, 128), BF16),
    rowbuf=pltpu.VMEM((RG, M, 128), BF16),
    colbuf=pltpu.VMEM((NROW, M, 128), BF16),
    t1=pltpu.VMEM((NROW, 1, 128), F32),
    t2=pltpu.VMEM((NSLOT, 1, 128), F32),
    tsrc=pltpu.VMEM((1, 128), F32),
    tvec=pltpu.VMEM((1, 128), F32),
    table=pltpu.VMEM((32, 128), F32),
    spread=pltpu.VMEM((128, NROW * M), BF16),
    wtab=pltpu.VMEM((4, 8, NROW * M), F32),
    a_op=pltpu.VMEM((SUPER, ROWS, 256), BF16),
    b_op=pltpu.VMEM((QUART, 2 * QCOLS, 256), BF16),
    f1=pltpu.VMEM((NROW * M, 256), BF16),
    f2=pltpu.VMEM((NROW * M, 256), BF16),
    f1t=pltpu.VMEM((208, RG * M), BF16),
    f2t=pltpu.VMEM((80, RG * M), BF16),
    colt=pltpu.VMEM((QUART, 128, QCOLS), F32),
    kmat=pltpu.VMEM((RG * M, NROW * M), BF16),
    cmat=pltpu.VMEM((RG * M, NROW * M), BF16),
    usum=pltpu.VMEM((SUPER, 8, NROW * M), F32),
    rowg=pltpu.VMEM((SUPER, 3, M, 128), F32),
    sibsend=pltpu.VMEM((SUPER, 3, M, 128), BF16),
    sibrecv=pltpu.VMEM((SUPER, 3, M, 128), BF16),
    rsend=pltpu.VMEM((CHUNKS - 1, M, 128), BF16),
    csend=pltpu.VMEM((NROW, M, 128), BF16),
    rowown=pltpu.VMEM((M, 128), F32),
    colown=pltpu.VMEM((M, 128), F32),
    rrow=pltpu.VMEM((CHUNKS - 1, M, 128), BF16),
    rcol=pltpu.VMEM((NROW - 1, M, 128), BF16),
    lossv=pltpu.VMEM((1, 128), F32),
    lsum=pltpu.VMEM((1, 128), F32),
    la=pltpu.VMEM((NCOL, 1, 128), F32),
    lb=pltpu.VMEM((NROW, 1, 128), F32),
)
SEND = dict(load=2, t1=1, t2=1, z=1, col=1, row=1, sib=1, sg=1, rr=1, rc=1, la=1, lb=1)
RECV = dict(t1=1, t2=1, z=3, col=QUART, row=SUPER, sib=SUPER, sg=SUPER, rr=1, rc=1, la=1, lb=1)


def kernel(samples, scores, groups, out, *rest):
    ref = Refs(SCRATCH, rest[:len(SCRATCH)])
    sems = rest[len(SCRATCH):]
    send = Refs(SEND, sems[:len(SEND)])
    recv = Refs(RECV, sems[len(SEND):])
    row, col = lax.axis_index("row"), lax.axis_index("col")
    zh, x = row // 4, lax.rem(row, 4)
    zl, y, core = col // 16, lax.rem(col // 2, 8), lax.rem(col, 2)
    sib = col + 1 - 2 * core

    def wrap(value, size):
        return jnp.where(value >= size, value - size, value)

    barrier = pltpu.get_barrier_semaphore()

    def greet(to_row, to_col):
        pl.semaphore_signal(barrier, inc=1, device_id=(to_row, to_col), device_id_type=MESH)

    for d in FAR_ROW:
        greet(wrap(row + d, NROW), col)
    for d in FAR_COL:
        greet(row, wrap(col + d, NCOL))

    loads = [pltpu.make_async_copy(samples, ref.xin, send.load.at[0]),
             pltpu.make_async_copy(scores, ref.sin, send.load.at[1])]
    for load in loads:
        load.start()
    town = groups[0, 0].astype(F32)
    tfull = jnp.full((1, 128), town, F32)
    ref.tsrc[...] = tfull
    ref.t1[0] = tfull
    expansion(ref, row, zh, x)
    for load in loads:
        load.wait()
    own = jnp.concatenate([ref.xin[...], ref.sin[...]], axis=1)
    ref.own[...] = own
    ref.rowbuf[RG - 4] = own
    ref.colbuf[12] = own
    pl.semaphore_wait(barrier, NROW + NCOL - 2)

    def copy(src, dst, ssem, rsem, to_row, to_col):
        return pltpu.make_async_remote_copy(
            src_ref=src, dst_ref=dst, send_sem=ssem, recv_sem=rsem,
            device_id=(to_row, to_col), device_id_type=MESH,
        )

    def t1_copy(d):
        return copy(ref.tsrc, ref.t1.at[NROW - d], send.t1.at[0], recv.t1.at[0], wrap(row + d, NROW), col)

    def t2_copy(t, b):
        chip = chip_at(zl, y, OFFSETS[t], -1)
        slot = 2 * (t - 1) + lax.rem(core + b, 2)
        return copy(ref.tvec, ref.t2.at[slot], send.t2.at[0], recv.t2.at[0], row, 2 * chip + b)

    def z_copy(quarter):
        to = wrap(zh + 3 - quarter, 4) * 4 + x
        return copy(ref.own, ref.colbuf.at[quarter * 4], send.z.at[0], recv.z.at[quarter], to, col)

    def col_copy(quarter, dx):
        to = zh * 4 + wrap(x + 4 - dx, 4)
        src = ref.own if quarter == 3 else ref.colbuf.at[quarter * 4]
        return copy(src, ref.colbuf.at[quarter * 4 + dx], send.col.at[0], recv.col.at[quarter], to, col)

    def row_copy(t):
        chip = chip_at(zl, y, OFFSETS[t], -1)
        slot = GROUPS * (t // 3) + t % 3
        return copy(ref.own, ref.rowbuf.at[slot], send.row.at[0], recv.row.at[t // 3], row, 2 * chip + core)

    def sib_copy(step):
        at = GROUPS * step
        return copy(ref.rowbuf.at[at:at + 3], ref.rowbuf.at[at + 3:at + 6], send.sib.at[0], recv.sib.at[step], row, sib)

    def sg_copy(step):
        return copy(ref.sibsend.at[step], ref.sibrecv.at[step], send.sg.at[0], recv.sg.at[step], row, sib)

    def rr_copy(t):
        chip = chip_at(zl, y, OFFSETS[t], 1)
        return copy(ref.rsend.at[t], ref.rrow.at[t], send.rr.at[0], recv.rr.at[0], row, 2 * chip + core)

    def rc_copy(quarter, dx):
        dz = (quarter + 1) % 4
        to = wrap(zh + dz, 4) * 4 + wrap(x + dx, 4)
        slot = quarter * 4 + dx - (1 if quarter == 3 else 0)
        return copy(ref.csend.at[quarter * 4 + dx], ref.rcol.at[slot], send.rc.at[0], recv.rc.at[0], to, col)

    def la_copy(d):
        return copy(ref.lossv, ref.la.at[NCOL - d], send.la.at[0], recv.la.at[0], row, wrap(col + d, NCOL))

    def lb_copy(d):
        return copy(ref.lsum, ref.lb.at[NROW - d], send.lb.at[0], recv.lb.at[0], wrap(row + d, NROW), col)

    def landed(buf, sem):
        copy(buf, buf, sem, sem, row, sib).wait_recv()

    def left(buf, sem):
        copy(buf, buf, sem, sem, row, sib).wait_send()

    for d in FAR_ROW:
        t1_copy(d).start()
    for quarter in (1, 0, 2):
        z_copy(quarter).start()
    for t in range(CHUNKS - 1):
        row_copy(t).start()
    for dx in (2, 1, 3):
        col_copy(3, dx).start()

    def got_z(quarter):
        landed(ref.colbuf.at[quarter * 4], recv.z.at[quarter])
        for dx in (2, 1, 3):
            col_copy(quarter, dx).start()

    def got_cols(quarter):
        at = quarter * 4
        landed(ref.colbuf.at[at + 1:at + 4], recv.col.at[quarter])
        prep_cols(ref, quarter)

    def got_rows(step):
        at = GROUPS * step
        landed(ref.rowbuf.at[at:at + (2 if step == 2 else 3)], recv.row.at[step])
        sib_copy(step).start()

    def got_sib(step):
        at = GROUPS * step
        landed(ref.rowbuf.at[at + 3:at + 6], recv.sib.at[step])
        prep_rows(ref, step)

    got_z(0)
    got_z(2)
    got_rows(2)
    got_z(1)
    landed(ref.t1.at[1:NROW], recv.t1.at[0])
    lane3 = lax.broadcasted_iota(jnp.int32, (NROW, 1, 128), 2)
    slot3 = lax.broadcasted_iota(jnp.int32, (NROW, 1, 128), 0)
    ref.tvec[...] = jnp.sum(jnp.where(lane3 == slot3, ref.t1[...], 0.0), axis=0)
    for t in range(1, CHUNKS - 1):
        for b in range(2):
            t2_copy(t, b).start()
    got_rows(1)
    got_rows(0)
    got_cols(3)
    got_sib(2)
    pair_step(ref, 2, 3)
    got_cols(0)
    pair_step(ref, 2, 0)
    got_sib(1)
    pair_step(ref, 1, 3)
    pair_step(ref, 1, 0)
    got_cols(2)
    pair_step(ref, 2, 2)
    pair_step(ref, 1, 2)
    got_sib(0)
    pair_step(ref, 0, 3)
    pair_step(ref, 0, 0)
    pair_step(ref, 0, 2)
    landed(ref.t2, recv.t2.at[0])
    pair_weights(ref, town, row)
    got_cols(1)
    for step in range(SUPER):
        pair_step(ref, step, 1)

    lane = lanes()
    own32 = ref.own[...].astype(F32)
    kept_diag = jnp.where((row // 2).astype(F32) < jnp.full((1, 128), town, F32), 1.0, 0.0)
    part = jnp.zeros((1, NROW * M), F32)
    for step in range(SUPER):
        part = part + jnp.sum(ref.usum[step, 0:GROUPS] * ref.wtab[step, 0:GROUPS], axis=0, keepdims=True)
    s2 = jnp.sum(jnp.where(lane < 64, 1.0 / 64, own32 * own32), axis=0, keepdims=True)
    loss = jnp.sum(part, axis=1, keepdims=True) - jnp.sum(s2 * kept_diag, axis=1, keepdims=True)
    count = tfull * (128.0 * 2048.0) - 64.0 * kept_diag
    lossv = jnp.where(lane == 0, loss, jnp.where(lane == 1, count, 0.0))
    ref.lossv[...] = lossv
    ref.la[0] = lossv
    for d in FAR_COL:
        la_copy(d).start()

    def cols_out(quarter):
        col_results(ref, quarter)
        for dx in (2, 1, 3, 0):
            if (quarter, dx) != (3, 0):
                rc_copy(quarter, dx).start()

    def rows_out(step):
        row_results(ref, step)
        sg_copy(step).start()

    def rows_on(step):
        landed(ref.sibrecv.at[step], recv.sg.at[step])
        both = ref.rowg[step] + ref.sibrecv[step].astype(F32)
        if step == SUPER - 1:
            ref.rsend[6:8] = both[0:2].astype(BF16)
            ref.rowown[...] = both[2]
        else:
            ref.rsend[3 * step:3 * step + 3] = both.astype(BF16)
        for t in range(3 * step, min(3 * step + 3, CHUNKS - 1)):
            rr_copy(t).start()

    rows_out(0)
    cols_out(1)
    rows_on(0)
    rows_out(1)
    cols_out(0)
    rows_on(1)
    cols_out(2)
    landed(ref.la.at[1:NCOL], recv.la.at[0])
    lsum = jnp.sum(ref.la[...], axis=0)
    ref.lsum[...] = lsum
    ref.lb[0] = lsum
    for d in FAR_ROW:
        lb_copy(d).start()
    rows_out(2)
    cols_out(3)
    rows_on(2)

    total = ref.rowown[...] + ref.colown[...] - jnp.where(lane < 64, 0.0, 2.0 * kept_diag * own32)
    landed(ref.rrow, recv.rr.at[0])
    total = total + jnp.sum(ref.rrow[...].astype(F32), axis=0)
    landed(ref.rcol, recv.rc.at[0])
    total = total + jnp.sum(ref.rcol[...].astype(F32), axis=0)

    landed(ref.lb.at[1:NROW], recv.lb.at[0])
    sums = jnp.sum(ref.lb[...], axis=0)
    pairs = sums[:, 1:2]
    out[0:64, :] = total * (EVERYONE / pairs)
    out[64:72, :] = jnp.broadcast_to(sums[:, 0:1] / pairs, (8, 128))

    left(ref.t1.at[1:NROW], send.t1.at[0])
    left(ref.t2, send.t2.at[0])
    left(ref.colbuf.at[0:3], send.z.at[0])
    left(ref.colbuf.at[0:12], send.col.at[0])
    left(ref.rrow, send.row.at[0])
    left(ref.rowbuf.at[0:CHUNKS], send.sib.at[0])
    left(ref.sibsend, send.sg.at[0])
    left(ref.rrow, send.rr.at[0])
    left(ref.rcol, send.rc.at[0])
    left(ref.la.at[1:NCOL], send.la.at[0])
    left(ref.lb.at[1:NROW], send.lb.at[0])


def shards(samples, scores, tile_groups):
    vmem = pl.BlockSpec(memory_space=pltpu.VMEM)
    hbm = pl.BlockSpec(memory_space=pltpu.HBM)
    out = pl.pallas_call(
        kernel,
        out_shape=jax.ShapeDtypeStruct((M + 8, 128), F32),
        in_specs=[hbm, hbm, pl.BlockSpec(memory_space=pltpu.SMEM)],
        out_specs=vmem,
        scratch_shapes=list(SCRATCH.values())
        + [pltpu.SemaphoreType.DMA((n,)) for n in (*SEND.values(), *RECV.values())],
        compiler_params=pltpu.CompilerParams(
            collective_id=0, has_side_effects=True, vmem_limit_bytes=64 * 2**20
        ),
    )(samples, scores, tile_groups)
    def split(whole, out_x, out_s, out_loss):
        out_x[...] = whole[0:M, 0:64]
        out_s[...] = whole[0:M, 64:128]
        out_loss[...] = whole[M:M + 1, 0:1]

    out_x, out_s, loss = pl.pallas_call(
        split,
        out_shape=(
            jax.ShapeDtypeStruct((M, 64), F32),
            jax.ShapeDtypeStruct((M, 64), F32),
            jax.ShapeDtypeStruct((1, 1), F32),
        ),
        in_specs=[vmem],
        out_specs=(vmem, vmem, vmem),
        compiler_params=pltpu.CompilerParams(vmem_limit_bytes=64 * 2**20),
    )(out)
    return out_x, out_s, loss[0, 0]


def solution(mesh):
    placed = (P(("row", "col"), None), P(("row", "col"), None), P("row", "col"))
    return jax.shard_map(
        shards,
        mesh=mesh,
        in_specs=placed,
        out_specs=(P(("row", "col"), None), P(("row", "col"), None), P()),
        check_vma=False,
    )
```

```python
import jax
import jax.numpy as jnp
from jax import lax
from jax.experimental import pallas as pl
from jax.experimental.pallas import tpu as pltpu
from jax.sharding import PartitionSpec as P

MESH = pl.DeviceIdType.MESH
F32 = jnp.float32
BF16 = jnp.bfloat16

NROW, NCOL = 16, 32
M = 64
CHUNKS = 9
RG = 2 * CHUNKS
SUPER = 3
GROUPS = RG // SUPER
ROWS = GROUPS * M
QUART = 4
QCOLS = 4 * M
EVERYONE = float(M * NROW * NCOL)
FAR_ROW = (10, 8, 9, 11, 6, 14, 4, 12, 5, 7, 13, 15, 2, 1, 3)
FAR_COL = tuple(sorted(range(1, 32), key=lambda d: -min((d // 2) % 8, 8 - (d // 2) % 8)))
NSLOT = 14

OFFSETS = (
    (0, 4, True), (0, 3, False), (1, -3, False),
    (1, None, False), (1, 2, False), (0, -2, False),
    (0, 1, False), (1, -1, False), (0, 0, True),
)


def split3(value):
    hi = value.astype(BF16).astype(F32)
    rest = value - hi
    mid = rest.astype(BF16).astype(F32)
    return hi, mid, rest - mid


def dot(a, b):
    return lax.dot_general(a, b, (((1,), (0,)), ((), ())), preferred_element_type=F32)


def dot_nt(a, b):
    return lax.dot_general(a, b, (((1,), (1,)), ((), ())), preferred_element_type=F32)


def lanes(rows=1, width=128):
    return lax.broadcasted_iota(jnp.int32, (rows, width), 1)


def squares(p, sw):
    q = p * jnp.where(lanes() < 64, p, sw)
    hi = q.astype(BF16)
    return jnp.concatenate([hi, (q - hi.astype(F32)).astype(BF16)], axis=1)


def sum_weights(e_lanes, s_lanes):
    k = lax.broadcasted_iota(jnp.int32, (256, 128), 0) % 128
    lane = lax.broadcasted_iota(jnp.int32, (256, 128), 1)
    is_x = k < 64
    out = jnp.zeros((256, 128), F32)
    if e_lanes is not None:
        in_e = (lane >= e_lanes) & (lane < e_lanes + 3)
        out = jnp.where(in_e & is_x, -(2.0 ** -7), out)
    if s_lanes is not None:
        in_s = (lane >= s_lanes) & (lane < s_lanes + 3)
        out = jnp.where(in_s, jnp.where(is_x, -(2.0 ** -18), 2.0 ** -12), out)
    return out.astype(BF16)


def pick3(value):
    hi, mid, lo = split3(value)
    part = lanes() % 3
    return jnp.where(part == 0, hi, jnp.where(part == 1, mid, lo))


def prep_rows(ref, step):
    pair = ref.rowbuf[pl.ds(step * GROUPS, GROUPS)].reshape(ROWS, 128)
    p = pair.astype(F32)
    sw = pltpu.roll(p, 64, 1)
    lane = lanes()
    sums = dot(squares(p, sw), sum_weights(0, 6))
    one = (((lane >= 3) & (lane < 6)) | (lane == 9)).astype(F32)
    misc = pick3(sums) + one
    ext = jnp.where(lane < 64, misc, p).astype(BF16)
    ref.a_op[step] = jnp.concatenate([pair, ext], axis=1)
    pt = p.T
    xt, st = pt[0:64], pt[64:128]
    ones = jnp.ones((16, ROWS), F32)
    at = pl.ds(step * ROWS, ROWS)
    ref.f1t[:, at] = jnp.concatenate([st * (-1.0 / 64), st, xt * (-1.0 / 64), ones], axis=0).astype(BF16)
    ref.f2t[:, at] = jnp.concatenate([xt, ones], axis=0).astype(BF16)


def prep_cols(ref, quarter):
    pair = ref.colbuf[pl.ds(quarter * 4, 4)].reshape(QCOLS, 128)
    p = pair.astype(F32)
    sw = pltpu.roll(p, 64, 1)
    lane = lanes()
    first = lane < 64
    sq = squares(p, sw)
    sums_e = dot(sq, sum_weights(3, None))
    sums_s = dot(sq, sum_weights(None, 3))
    u = p * jnp.where(first, 2.0 ** -17, 2.0 ** -6) - sw * (2.0 ** -12)
    u_hi = u.astype(BF16)
    e1 = jnp.where(first, p * (1.0 / 64), 0.0).astype(BF16)
    e2 = pick3(sums_e) + (lane < 3).astype(F32)
    s2 = pick3(sums_s) + ((lane >= 6) & (lane < 9)).astype(F32) + jnp.where(lane == 9, 33.0 / 2048, 0.0)
    s2 = jnp.where(first, s2, u - u_hi.astype(F32))
    ref.b_op[quarter, 0:QCOLS, :] = jnp.concatenate([e1, e2.astype(BF16)], axis=1)
    ref.b_op[quarter, QCOLS:2 * QCOLS, :] = jnp.concatenate([u_hi, s2.astype(BF16)], axis=1)
    sw64 = sw * (-1.0 / 64)
    f1a = jnp.where(first, sw64, p)
    f1b = jnp.where(first, (lane == 0).astype(F32), sw64)
    f2a = jnp.where(first, p, 0.0)
    f2b = jnp.broadcast_to((lane == 1).astype(F32), p.shape)
    at = pl.ds(quarter * QCOLS, QCOLS)
    ref.f1[at, :] = jnp.concatenate([f1a, f1b], axis=1).astype(BF16)
    ref.f2[at, :] = jnp.concatenate([f2a, f2b], axis=1).astype(BF16)
    ref.colt[quarter] = p.T


def pair_step(ref, step, quarter):
    es = dot_nt(ref.a_op[step], ref.b_op[quarter])
    kept = jnp.exp(es[:, :QCOLS])
    coef = kept * es[:, QCOLS:]
    at = (pl.ds(step * ROWS, ROWS), slice(quarter * QCOLS, (quarter + 1) * QCOLS))
    ref.kmat[at] = kept.astype(BF16)
    ref.cmat[at] = coef.astype(BF16)
    to = (step, slice(0, GROUPS), slice(quarter * QCOLS, (quarter + 1) * QCOLS))
    ref.usum[to] = jnp.sum((coef * 64.0 - kept * (1.0 / 32)).reshape(GROUPS, M, QCOLS), axis=1)


def expansion(ref, row, zh, x):
    lane = lanes(1, NROW * M)
    slot = lane // M
    quarter, dx = slot // 4, slot % 4
    other = ((zh + quarter + 1) % 4) * 4 + (x + dx) % 4
    place = (other - row + NROW) % NROW
    hot = (lax.broadcasted_iota(jnp.int32, (NROW, NROW * M), 0) == place).astype(F32)
    ref.spread[...] = jnp.concatenate([hot, jnp.zeros((128 - NROW, NROW * M), F32)], axis=0).astype(BF16)


def pair_weights(ref, town, row):
    lane = lanes()
    theirs = ((row + lane) % NROW) // 2
    k12 = (theirs.astype(F32) < town).astype(F32)
    half = (row // 2).astype(F32)
    ref.table[...] = jnp.zeros_like(ref.table)
    for step in range(SUPER):
        for i in range(GROUPS):
            rel, t = i // 3, 3 * step + i % 3
            weight = k12
            if not OFFSETS[t][2]:
                weight = k12 + (half < ref.t2[2 * (t - 1) + rel]).astype(F32)
            ref.table[8 * step + i:8 * step + i + 1, :] = weight
    ref.wtab[...] = dot(ref.table[...].astype(BF16), ref.spread[...]).reshape(4, 8, NROW * M)


def weighted(mat, ref, step, start, width):
    at = slice(start, start + width)
    out = []
    for i in range(GROUPS):
        w = jnp.broadcast_to(ref.wtab[step, i:i + 1, at], (16, width)).astype(BF16)
        part = mat[step * ROWS + i * M:step * ROWS + (i + 1) * M, at]
        out.append(part * jnp.concatenate([w] * (M // 16), axis=0))
    return jnp.concatenate(out, axis=0)


def row_results(ref, step):
    kb = weighted(ref.kmat, ref, step, 0, NROW * M)
    cb = weighted(ref.cmat, ref, step, 0, NROW * M)
    acc = dot(kb, ref.f1[...]) + dot(cb, ref.f2[...])
    low, high = acc[:, :128], acc[:, 128:]
    ks, cs = high[:, 0:1], high[:, 1:2]
    p = ref.rowbuf[step * GROUPS:(step + 1) * GROUPS].reshape(ROWS, 128).astype(F32)
    sw = pltpu.roll(p, 64, 1)
    grad = low + jnp.where(lanes() < 64, p * (-cs), high) + sw * (ks * (1.0 / 64))
    grad = grad.reshape(GROUPS, M, 128)
    ref.rowg[step] = grad[0:3]
    ref.sibsend[step] = grad[3:6].astype(BF16)


def col_results(ref, quarter):
    kb = jnp.concatenate([weighted(ref.kmat, ref, s, quarter * QCOLS, QCOLS) for s in range(SUPER)], axis=0)
    cb = jnp.concatenate([weighted(ref.cmat, ref, s, quarter * QCOLS, QCOLS) for s in range(SUPER)], axis=0)
    g1 = dot(ref.f1t[...], kb)
    g2 = dot(ref.f2t[...], cb)
    pt = ref.colt[quarter]
    xt, st = pt[0:64], pt[64:128]
    ks = g1[192:193] * (1.0 / 64)
    cs = g2[64:65]
    gx = g2[0:64] + g1[0:64] - xt * cs + st * ks
    gs = g1[64:128] + g1[128:192] + xt * ks
    grad = jnp.concatenate([gx, gs], axis=0).T.reshape(4, M, 128)
    ref.csend[quarter * 4:quarter * 4 + 4] = grad.astype(BF16)
    ref.colown[quarter] = grad[0]


def chip_at(zl, y, offset, sign):
    other, dy, _ = offset
    z = lax.rem(zl + other, 2)
    if dy is None:
        from_z = zl if sign > 0 else z
        dy = 4 * from_z
    return z * 8 + lax.rem(y + sign * dy + 16, 8)


class Refs:
    def __init__(self, names, refs):
        for name, r in zip(names, refs):
            setattr(self, name, r)


SCRATCH = dict(
    xin=pltpu.VMEM((M, 64), BF16),
    sin=pltpu.VMEM((M, 64), BF16),
    own=pltpu.VMEM((M, 128), BF16),
    rowbuf=pltpu.VMEM((RG, M, 128), BF16),
    colbuf=pltpu.VMEM((NROW, M, 128), BF16),
    t1=pltpu.VMEM((NROW, 1, 128), F32),
    t2=pltpu.VMEM((NSLOT, 1, 128), F32),
    tsrc=pltpu.VMEM((1, 128), F32),
    tvec=pltpu.VMEM((1, 128), F32),
    table=pltpu.VMEM((32, 128), F32),
    spread=pltpu.VMEM((128, NROW * M), BF16),
    wtab=pltpu.VMEM((4, 8, NROW * M), F32),
    a_op=pltpu.VMEM((SUPER, ROWS, 256), BF16),
    b_op=pltpu.VMEM((QUART, 2 * QCOLS, 256), BF16),
    f1=pltpu.VMEM((NROW * M, 256), BF16),
    f2=pltpu.VMEM((NROW * M, 256), BF16),
    f1t=pltpu.VMEM((208, RG * M), BF16),
    f2t=pltpu.VMEM((80, RG * M), BF16),
    colt=pltpu.VMEM((QUART, 128, QCOLS), F32),
    kmat=pltpu.VMEM((RG * M, NROW * M), BF16),
    cmat=pltpu.VMEM((RG * M, NROW * M), BF16),
    usum=pltpu.VMEM((SUPER, 8, NROW * M), F32),
    rowg=pltpu.VMEM((SUPER, 3, M, 128), F32),
    sibsend=pltpu.VMEM((SUPER, 3, M, 128), BF16),
    sibrecv=pltpu.VMEM((SUPER, 3, M, 128), BF16),
    rsend=pltpu.VMEM((CHUNKS - 1, M, 128), BF16),
    csend=pltpu.VMEM((NROW, M, 128), BF16),
    rowown=pltpu.VMEM((M, 128), F32),
    colown=pltpu.VMEM((QUART, M, 128), F32),
    xrecv=pltpu.VMEM((2, 3, M, 128), BF16),
    zsend=pltpu.VMEM((2, M, 128), BF16),
    rrow=pltpu.VMEM((CHUNKS - 1, M, 128), BF16),
    rcol=pltpu.VMEM((9, M, 128), BF16),
    lossv=pltpu.VMEM((1, 128), F32),
    lsum=pltpu.VMEM((1, 128), F32),
    la=pltpu.VMEM((NCOL, 1, 128), F32),
    lb=pltpu.VMEM((NROW, 1, 128), F32),
)
SEND = dict(load=2, t1=1, t2=1, z=1, col=1, row=1, sib=1, sg=1, rr=1, rc=1, xs=1, la=1, lb=1)
RECV = dict(t1=1, t2=1, z=3, col=QUART, row=SUPER, sib=SUPER, sg=SUPER, rr=1, rc=1, xs=2, la=1, lb=1)


def kernel(samples, scores, groups, out, *rest):
    ref = Refs(SCRATCH, rest[:len(SCRATCH)])
    sems = rest[len(SCRATCH):]
    send = Refs(SEND, sems[:len(SEND)])
    recv = Refs(RECV, sems[len(SEND):])
    row, col = lax.axis_index("row"), lax.axis_index("col")
    zh, x = row // 4, lax.rem(row, 4)
    zl, y, core = col // 16, lax.rem(col // 2, 8), lax.rem(col, 2)
    sib = col + 1 - 2 * core

    def wrap(value, size):
        return jnp.where(value >= size, value - size, value)

    barrier = pltpu.get_barrier_semaphore()

    def greet(to_row, to_col):
        pl.semaphore_signal(barrier, inc=1, device_id=(to_row, to_col), device_id_type=MESH)

    for d in FAR_ROW:
        greet(wrap(row + d, NROW), col)
    for d in FAR_COL:
        greet(row, wrap(col + d, NCOL))

    loads = [pltpu.make_async_copy(samples, ref.xin, send.load.at[0]),
             pltpu.make_async_copy(scores, ref.sin, send.load.at[1])]
    for load in loads:
        load.start()
    town = groups[0, 0].astype(F32)
    tfull = jnp.full((1, 128), town, F32)
    ref.tsrc[...] = tfull
    ref.t1[0] = tfull
    expansion(ref, row, zh, x)
    for load in loads:
        load.wait()
    own = jnp.concatenate([ref.xin[...], ref.sin[...]], axis=1)
    ref.own[...] = own
    ref.rowbuf[RG - 4] = own
    ref.colbuf[12] = own
    pl.semaphore_wait(barrier, NROW + NCOL - 2)

    def copy(src, dst, ssem, rsem, to_row, to_col):
        return pltpu.make_async_remote_copy(
            src_ref=src, dst_ref=dst, send_sem=ssem, recv_sem=rsem,
            device_id=(to_row, to_col), device_id_type=MESH,
        )

    def t1_copy(d):
        return copy(ref.tsrc, ref.t1.at[NROW - d], send.t1.at[0], recv.t1.at[0], wrap(row + d, NROW), col)

    def t2_copy(t, b):
        chip = chip_at(zl, y, OFFSETS[t], -1)
        slot = 2 * (t - 1) + lax.rem(core + b, 2)
        return copy(ref.tvec, ref.t2.at[slot], send.t2.at[0], recv.t2.at[0], row, 2 * chip + b)

    def z_copy(quarter):
        to = wrap(zh + 3 - quarter, 4) * 4 + x
        return copy(ref.own, ref.colbuf.at[quarter * 4], send.z.at[0], recv.z.at[quarter], to, col)

    def col_copy(quarter, dx):
        to = zh * 4 + wrap(x + 4 - dx, 4)
        src = ref.own if quarter == 3 else ref.colbuf.at[quarter * 4]
        return copy(src, ref.colbuf.at[quarter * 4 + dx], send.col.at[0], recv.col.at[quarter], to, col)

    def row_copy(t):
        chip = chip_at(zl, y, OFFSETS[t], -1)
        slot = GROUPS * (t // 3) + t % 3
        return copy(ref.own, ref.rowbuf.at[slot], send.row.at[0], recv.row.at[t // 3], row, 2 * chip + core)

    def sib_copy(step):
        at = GROUPS * step
        return copy(ref.rowbuf.at[at:at + 3], ref.rowbuf.at[at + 3:at + 6], send.sib.at[0], recv.sib.at[step], row, sib)

    def sg_copy(step):
        return copy(ref.sibsend.at[step], ref.sibrecv.at[step], send.sg.at[0], recv.sg.at[step], row, sib)

    def rr_copy(t):
        chip = chip_at(zl, y, OFFSETS[t], 1)
        return copy(ref.rsend.at[t], ref.rrow.at[t], send.rr.at[0], recv.rr.at[0], row, 2 * chip + core)

    def rc_copy(quarter, dx):
        src = ref.csend.at[quarter * 4 + dx]
        to_x = wrap(x + dx, 4)
        if quarter == 1:
            return copy(src, ref.rcol.at[dx], send.rc.at[0], recv.rc.at[0], wrap(zh + 2, 4) * 4 + to_x, col)
        if quarter == 3:
            return copy(src, ref.rcol.at[3 + dx], send.rc.at[0], recv.rc.at[0], zh * 4 + to_x, col)
        half = quarter // 2
        return copy(src, ref.xrecv.at[half, dx - 1], send.xs.at[0], recv.xs.at[half], zh * 4 + to_x, col)

    def zs_copy(quarter):
        to = wrap(zh + quarter + 1, 4) * 4 + x
        return copy(ref.zsend.at[quarter // 2], ref.rcol.at[7 + quarter // 2], send.rc.at[0], recv.rc.at[0], to, col)

    def la_copy(d):
        return copy(ref.lossv, ref.la.at[NCOL - d], send.la.at[0], recv.la.at[0], row, wrap(col + d, NCOL))

    def lb_copy(d):
        return copy(ref.lsum, ref.lb.at[NROW - d], send.lb.at[0], recv.lb.at[0], wrap(row + d, NROW), col)

    def landed(buf, sem):
        copy(buf, buf, sem, sem, row, sib).wait_recv()

    def left(buf, sem):
        copy(buf, buf, sem, sem, row, sib).wait_send()

    for d in FAR_ROW:
        t1_copy(d).start()
    for quarter in (1, 0, 2):
        z_copy(quarter).start()
    for t in range(CHUNKS - 1):
        row_copy(t).start()
    for dx in (2, 1, 3):
        col_copy(3, dx).start()

    def got_z(quarter):
        landed(ref.colbuf.at[quarter * 4], recv.z.at[quarter])
        for dx in (2, 1, 3):
            col_copy(quarter, dx).start()

    def got_cols(quarter):
        at = quarter * 4
        landed(ref.colbuf.at[at + 1:at + 4], recv.col.at[quarter])
        prep_cols(ref, quarter)

    def got_rows(step):
        at = GROUPS * step
        landed(ref.rowbuf.at[at:at + (2 if step == 2 else 3)], recv.row.at[step])
        sib_copy(step).start()

    def got_sib(step):
        at = GROUPS * step
        landed(ref.rowbuf.at[at + 3:at + 6], recv.sib.at[step])
        prep_rows(ref, step)

    got_z(0)
    got_z(2)
    got_rows(2)
    got_z(1)
    landed(ref.t1.at[1:NROW], recv.t1.at[0])
    lane3 = lax.broadcasted_iota(jnp.int32, (NROW, 1, 128), 2)
    slot3 = lax.broadcasted_iota(jnp.int32, (NROW, 1, 128), 0)
    ref.tvec[...] = jnp.sum(jnp.where(lane3 == slot3, ref.t1[...], 0.0), axis=0)
    for t in range(1, CHUNKS - 1):
        for b in range(2):
            t2_copy(t, b).start()
    got_rows(1)
    got_rows(0)
    got_cols(3)
    got_sib(2)
    pair_step(ref, 2, 3)
    got_cols(0)
    pair_step(ref, 2, 0)
    got_sib(1)
    pair_step(ref, 1, 3)
    pair_step(ref, 1, 0)
    got_cols(2)
    pair_step(ref, 2, 2)
    pair_step(ref, 1, 2)
    got_sib(0)
    pair_step(ref, 0, 3)
    pair_step(ref, 0, 0)
    pair_step(ref, 0, 2)
    landed(ref.t2, recv.t2.at[0])
    pair_weights(ref, town, row)
    got_cols(1)
    for step in range(SUPER):
        pair_step(ref, step, 1)

    lane = lanes()
    own32 = ref.own[...].astype(F32)
    kept_diag = jnp.where((row // 2).astype(F32) < jnp.full((1, 128), town, F32), 1.0, 0.0)
    part = jnp.zeros((1, NROW * M), F32)
    for step in range(SUPER):
        part = part + jnp.sum(ref.usum[step, 0:GROUPS] * ref.wtab[step, 0:GROUPS], axis=0, keepdims=True)
    s2 = jnp.sum(jnp.where(lane < 64, 1.0 / 64, own32 * own32), axis=0, keepdims=True)
    loss = jnp.sum(part, axis=1, keepdims=True) - jnp.sum(s2 * kept_diag, axis=1, keepdims=True)
    count = tfull * (128.0 * 2048.0) - 64.0 * kept_diag
    lossv = jnp.where(lane == 0, loss, jnp.where(lane == 1, count, 0.0))
    ref.lossv[...] = lossv
    ref.la[0] = lossv
    for d in FAR_COL:
        la_copy(d).start()

    def cols_out(quarter):
        col_results(ref, quarter)
        for dx in (2, 1, 3, 0):
            if quarter == 1 or dx:
                rc_copy(quarter, dx).start()

    def cols_on(quarter):
        half = quarter // 2
        landed(ref.xrecv.at[half], recv.xs.at[half])
        both = ref.colown[quarter] + jnp.sum(ref.xrecv[half].astype(F32), axis=0)
        ref.zsend[half] = both.astype(BF16)
        zs_copy(quarter).start()

    def rows_out(step):
        row_results(ref, step)
        sg_copy(step).start()

    def rows_on(step):
        landed(ref.sibrecv.at[step], recv.sg.at[step])
        both = ref.rowg[step] + ref.sibrecv[step].astype(F32)
        if step == SUPER - 1:
            ref.rsend[6:8] = both[0:2].astype(BF16)
            ref.rowown[...] = both[2]
        else:
            ref.rsend[3 * step:3 * step + 3] = both.astype(BF16)
        for t in range(3 * step, min(3 * step + 3, CHUNKS - 1)):
            rr_copy(t).start()

    rows_out(0)
    cols_out(1)
    cols_out(0)
    cols_out(2)
    rows_on(0)
    rows_out(1)
    cols_out(3)
    rows_on(1)
    rows_out(2)
    rows_on(2)
    landed(ref.la.at[1:NCOL], recv.la.at[0])
    lsum = jnp.sum(ref.la[...], axis=0)
    ref.lsum[...] = lsum
    ref.lb[0] = lsum
    for d in FAR_ROW:
        lb_copy(d).start()
    cols_on(0)
    cols_on(2)

    total = ref.rowown[...] + ref.colown[3] - jnp.where(lane < 64, 0.0, 2.0 * kept_diag * own32)
    landed(ref.rrow, recv.rr.at[0])
    total = total + jnp.sum(ref.rrow[...].astype(F32), axis=0)
    landed(ref.rcol, recv.rc.at[0])
    total = total + jnp.sum(ref.rcol[...].astype(F32), axis=0)

    landed(ref.lb.at[1:NROW], recv.lb.at[0])
    sums = jnp.sum(ref.lb[...], axis=0)
    pairs = sums[:, 1:2]
    out[0:64, :] = total * (EVERYONE / pairs)
    out[64:72, :] = jnp.broadcast_to(sums[:, 0:1] / pairs, (8, 128))

    left(ref.t1.at[1:NROW], send.t1.at[0])
    left(ref.t2, send.t2.at[0])
    left(ref.colbuf.at[0:3], send.z.at[0])
    left(ref.colbuf.at[0:12], send.col.at[0])
    left(ref.rrow, send.row.at[0])
    left(ref.rowbuf.at[0:CHUNKS], send.sib.at[0])
    left(ref.sibsend, send.sg.at[0])
    left(ref.rrow, send.rr.at[0])
    left(ref.rcol, send.rc.at[0])
    left(ref.xrecv, send.xs.at[0])
    left(ref.la.at[1:NCOL], send.la.at[0])
    left(ref.lb.at[1:NROW], send.lb.at[0])


def shards(samples, scores, tile_groups):
    vmem = pl.BlockSpec(memory_space=pltpu.VMEM)
    hbm = pl.BlockSpec(memory_space=pltpu.HBM)
    out = pl.pallas_call(
        kernel,
        out_shape=jax.ShapeDtypeStruct((M + 8, 128), F32),
        in_specs=[hbm, hbm, pl.BlockSpec(memory_space=pltpu.SMEM)],
        out_specs=vmem,
        scratch_shapes=list(SCRATCH.values())
        + [pltpu.SemaphoreType.DMA((n,)) for n in (*SEND.values(), *RECV.values())],
        compiler_params=pltpu.CompilerParams(
            collective_id=0, has_side_effects=True, vmem_limit_bytes=64 * 2**20
        ),
    )(samples, scores, tile_groups)
    def split(whole, out_x, out_s, out_loss):
        out_x[...] = whole[0:M, 0:64]
        out_s[...] = whole[0:M, 64:128]
        out_loss[...] = whole[M:M + 1, 0:1]

    out_x, out_s, loss = pl.pallas_call(
        split,
        out_shape=(
            jax.ShapeDtypeStruct((M, 64), F32),
            jax.ShapeDtypeStruct((M, 64), F32),
            jax.ShapeDtypeStruct((1, 1), F32),
        ),
        in_specs=[vmem],
        out_specs=(vmem, vmem, vmem),
        compiler_params=pltpu.CompilerParams(vmem_limit_bytes=64 * 2**20),
    )(out)
    return out_x, out_s, loss[0, 0]


def solution(mesh):
    placed = (P(("row", "col"), None), P(("row", "col"), None), P("row", "col"))
    return jax.shard_map(
        shards,
        mesh=mesh,
        in_specs=placed,
        out_specs=(P(("row", "col"), None), P(("row", "col"), None), P()),
        check_vma=False,
    )
```

```python
import jax
import jax.numpy as jnp
from jax import lax
from jax.experimental import pallas as pl
from jax.experimental.pallas import tpu as pltpu
from jax.sharding import PartitionSpec as P

MESH = pl.DeviceIdType.MESH
F32 = jnp.float32
BF16 = jnp.bfloat16

NROW, NCOL = 16, 32
M = 64
CHUNKS = 9
RG = 2 * CHUNKS
SUPER = 3
GROUPS = RG // SUPER
ROWS = GROUPS * M
QUART = 4
QCOLS = 4 * M
EVERYONE = float(M * NROW * NCOL)
FAR_ROW = (10, 8, 9, 11, 6, 14, 4, 12, 5, 7, 13, 15, 2, 1, 3)
FAR_COL = tuple(sorted(range(1, 32), key=lambda d: -min((d // 2) % 8, 8 - (d // 2) % 8)))
NSLOT = 14

OFFSETS = (
    (0, 4, True), (0, 3, False), (1, -3, False),
    (1, None, False), (1, 2, False), (0, -2, False),
    (0, 1, False), (1, -1, False), (0, 0, True),
)


def split3(value):
    hi = value.astype(BF16).astype(F32)
    rest = value - hi
    mid = rest.astype(BF16).astype(F32)
    return hi, mid, rest - mid


def dot(a, b):
    return lax.dot_general(a, b, (((1,), (0,)), ((), ())), preferred_element_type=F32)


def dot_nt(a, b):
    return lax.dot_general(a, b, (((1,), (1,)), ((), ())), preferred_element_type=F32)


def lanes(rows=1, width=128):
    return lax.broadcasted_iota(jnp.int32, (rows, width), 1)


def squares(p, sw):
    q = p * jnp.where(lanes() < 64, p, sw)
    hi = q.astype(BF16)
    return jnp.concatenate([hi, (q - hi.astype(F32)).astype(BF16)], axis=1)


def sum_weights(e_lanes, s_lanes):
    k = lax.broadcasted_iota(jnp.int32, (256, 128), 0) % 128
    lane = lax.broadcasted_iota(jnp.int32, (256, 128), 1)
    is_x = k < 64
    out = jnp.zeros((256, 128), F32)
    if e_lanes is not None:
        in_e = (lane >= e_lanes) & (lane < e_lanes + 3)
        out = jnp.where(in_e & is_x, -(2.0 ** -7), out)
    if s_lanes is not None:
        in_s = (lane >= s_lanes) & (lane < s_lanes + 3)
        out = jnp.where(in_s, jnp.where(is_x, -(2.0 ** -18), 2.0 ** -12), out)
    return out.astype(BF16)


def pick3(value):
    hi, mid, lo = split3(value)
    part = lanes() % 3
    return jnp.where(part == 0, hi, jnp.where(part == 1, mid, lo))


def prep_rows(ref, step):
    pair = ref.rowbuf[pl.ds(step * GROUPS, GROUPS)].reshape(ROWS, 128)
    p = pair.astype(F32)
    sw = pltpu.roll(p, 64, 1)
    lane = lanes()
    sums = dot(squares(p, sw), sum_weights(0, 6))
    one = (((lane >= 3) & (lane < 6)) | (lane == 9)).astype(F32)
    misc = pick3(sums) + one
    ext = jnp.where(lane < 64, misc, p).astype(BF16)
    ref.a_op[step] = jnp.concatenate([pair, ext], axis=1)
    pt = p.T
    xt, st = pt[0:64], pt[64:128]
    ones = jnp.ones((16, ROWS), F32)
    at = pl.ds(step * ROWS, ROWS)
    ref.f1t[:, at] = jnp.concatenate([st * (-1.0 / 64), st, xt * (-1.0 / 64), ones], axis=0).astype(BF16)
    ref.f2t[:, at] = jnp.concatenate([xt, ones], axis=0).astype(BF16)


def prep_cols(ref, quarter):
    pair = ref.colbuf[pl.ds(quarter * 4, 4)].reshape(QCOLS, 128)
    p = pair.astype(F32)
    sw = pltpu.roll(p, 64, 1)
    lane = lanes()
    first = lane < 64
    sq = squares(p, sw)
    sums_e = dot(sq, sum_weights(3, None))
    sums_s = dot(sq, sum_weights(None, 3))
    u = p * jnp.where(first, 2.0 ** -17, 2.0 ** -6) - sw * (2.0 ** -12)
    u_hi = u.astype(BF16)
    e1 = jnp.where(first, p * (1.0 / 64), 0.0).astype(BF16)
    e2 = pick3(sums_e) + (lane < 3).astype(F32)
    s2 = pick3(sums_s) + ((lane >= 6) & (lane < 9)).astype(F32) + jnp.where(lane == 9, 33.0 / 2048, 0.0)
    s2 = jnp.where(first, s2, u - u_hi.astype(F32))
    ref.b_op[quarter, 0:QCOLS, :] = jnp.concatenate([e1, e2.astype(BF16)], axis=1)
    ref.b_op[quarter, QCOLS:2 * QCOLS, :] = jnp.concatenate([u_hi, s2.astype(BF16)], axis=1)
    sw64 = sw * (-1.0 / 64)
    f1a = jnp.where(first, sw64, p)
    f1b = jnp.where(first, (lane == 0).astype(F32), sw64)
    f2a = jnp.where(first, p, 0.0)
    f2b = jnp.broadcast_to((lane == 1).astype(F32), p.shape)
    at = pl.ds(quarter * QCOLS, QCOLS)
    ref.f1[at, :] = jnp.concatenate([f1a, f1b], axis=1).astype(BF16)
    ref.f2[at, :] = jnp.concatenate([f2a, f2b], axis=1).astype(BF16)
    ref.colt[quarter] = p.T


def pair_step(ref, step, quarter):
    es = dot_nt(ref.a_op[step], ref.b_op[quarter])
    kept = jnp.exp(es[:, :QCOLS])
    coef = kept * es[:, QCOLS:]
    at = (pl.ds(step * ROWS, ROWS), slice(quarter * QCOLS, (quarter + 1) * QCOLS))
    ref.kmat[at] = kept.astype(BF16)
    ref.cmat[at] = coef.astype(BF16)
    to = (step, slice(0, GROUPS), slice(quarter * QCOLS, (quarter + 1) * QCOLS))
    ref.usum[to] = jnp.sum((coef * 64.0 - kept * (1.0 / 32)).reshape(GROUPS, M, QCOLS), axis=1)


def expansion(ref, row, zh, x):
    lane = lanes(1, NROW * M)
    slot = lane // M
    quarter, dx = slot // 4, slot % 4
    other = ((zh + quarter + 1) % 4) * 4 + (x + dx) % 4
    place = (other - row + NROW) % NROW
    hot = (lax.broadcasted_iota(jnp.int32, (NROW, NROW * M), 0) == place).astype(F32)
    ref.spread[...] = jnp.concatenate([hot, jnp.zeros((128 - NROW, NROW * M), F32)], axis=0).astype(BF16)


def pair_weights(ref, town, row):
    lane = lanes()
    theirs = ((row + lane) % NROW) // 2
    k12 = (theirs.astype(F32) < town).astype(F32)
    half = (row // 2).astype(F32)
    ref.table[...] = jnp.zeros_like(ref.table)
    for step in range(SUPER):
        for i in range(GROUPS):
            rel, t = i // 3, 3 * step + i % 3
            weight = k12
            if not OFFSETS[t][2]:
                weight = k12 + (half < ref.t2[2 * (t - 1) + rel]).astype(F32)
            ref.table[8 * step + i:8 * step + i + 1, :] = weight
    ref.wtab[...] = dot(ref.table[...].astype(BF16), ref.spread[...]).reshape(4, 8, NROW * M)


def weighted(mat, ref, step, start, width):
    at = slice(start, start + width)
    out = []
    for i in range(GROUPS):
        w = jnp.broadcast_to(ref.wtab[step, i:i + 1, at], (16, width)).astype(BF16)
        part = mat[step * ROWS + i * M:step * ROWS + (i + 1) * M, at]
        out.append(part * jnp.concatenate([w] * (M // 16), axis=0))
    return jnp.concatenate(out, axis=0)


def row_results(ref, step):
    kb = weighted(ref.kmat, ref, step, 0, NROW * M)
    cb = weighted(ref.cmat, ref, step, 0, NROW * M)
    acc = dot(kb, ref.f1[...]) + dot(cb, ref.f2[...])
    low, high = acc[:, :128], acc[:, 128:]
    ks, cs = high[:, 0:1], high[:, 1:2]
    p = ref.rowbuf[step * GROUPS:(step + 1) * GROUPS].reshape(ROWS, 128).astype(F32)
    sw = pltpu.roll(p, 64, 1)
    grad = low + jnp.where(lanes() < 64, p * (-cs), high) + sw * (ks * (1.0 / 64))
    grad = grad.reshape(GROUPS, M, 128)
    ref.rowg[step] = grad[0:3]
    ref.sibsend[step] = grad[3:6]


def col_results(ref, quarter):
    kb = jnp.concatenate([weighted(ref.kmat, ref, s, quarter * QCOLS, QCOLS) for s in range(SUPER)], axis=0)
    cb = jnp.concatenate([weighted(ref.cmat, ref, s, quarter * QCOLS, QCOLS) for s in range(SUPER)], axis=0)
    g1 = dot(ref.f1t[...], kb)
    g2 = dot(ref.f2t[...], cb)
    pt = ref.colt[quarter]
    xt, st = pt[0:64], pt[64:128]
    ks = g1[192:193] * (1.0 / 64)
    cs = g2[64:65]
    gx = g2[0:64] + g1[0:64] - xt * cs + st * ks
    gs = g1[64:128] + g1[128:192] + xt * ks
    grad = jnp.concatenate([gx, gs], axis=0).T.reshape(4, M, 128)
    ref.csend[quarter * 4:quarter * 4 + 4] = grad.astype(BF16)
    ref.colown[quarter] = grad[0]


def chip_at(zl, y, offset, sign):
    other, dy, _ = offset
    z = lax.rem(zl + other, 2)
    if dy is None:
        from_z = zl if sign > 0 else z
        dy = 4 * from_z
    return z * 8 + lax.rem(y + sign * dy + 16, 8)


class Refs:
    def __init__(self, names, refs):
        for name, r in zip(names, refs):
            setattr(self, name, r)


SCRATCH = dict(
    xin=pltpu.VMEM((M, 64), BF16),
    sin=pltpu.VMEM((M, 64), BF16),
    own=pltpu.VMEM((M, 128), BF16),
    rowbuf=pltpu.VMEM((RG, M, 128), BF16),
    colbuf=pltpu.VMEM((NROW, M, 128), BF16),
    t1=pltpu.VMEM((NROW, 1, 128), F32),
    t2=pltpu.VMEM((NSLOT, 1, 128), F32),
    tsrc=pltpu.VMEM((1, 128), F32),
    tvec=pltpu.VMEM((1, 128), F32),
    table=pltpu.VMEM((32, 128), F32),
    spread=pltpu.VMEM((128, NROW * M), BF16),
    wtab=pltpu.VMEM((4, 8, NROW * M), F32),
    a_op=pltpu.VMEM((SUPER, ROWS, 256), BF16),
    b_op=pltpu.VMEM((QUART, 2 * QCOLS, 256), BF16),
    f1=pltpu.VMEM((NROW * M, 256), BF16),
    f2=pltpu.VMEM((NROW * M, 256), BF16),
    f1t=pltpu.VMEM((208, RG * M), BF16),
    f2t=pltpu.VMEM((80, RG * M), BF16),
    colt=pltpu.VMEM((QUART, 128, QCOLS), F32),
    kmat=pltpu.VMEM((RG * M, NROW * M), BF16),
    cmat=pltpu.VMEM((RG * M, NROW * M), BF16),
    usum=pltpu.VMEM((SUPER, 8, NROW * M), F32),
    rowg=pltpu.VMEM((SUPER, 3, M, 128), F32),
    sibsend=pltpu.VMEM((SUPER, 3, M, 128), F32),
    sibrecv=pltpu.VMEM((SUPER, 3, M, 128), F32),
    rsend=pltpu.VMEM((CHUNKS - 1, M, 128), BF16),
    csend=pltpu.VMEM((NROW, M, 128), BF16),
    rowown=pltpu.VMEM((M, 128), F32),
    colown=pltpu.VMEM((QUART, M, 128), F32),
    xrecv=pltpu.VMEM((2, 3, M, 128), BF16),
    zsend=pltpu.VMEM((2, M, 128), BF16),
    rrow=pltpu.VMEM((CHUNKS - 1, M, 128), BF16),
    rcol=pltpu.VMEM((9, M, 128), BF16),
    lossv=pltpu.VMEM((1, 128), F32),
    lsum=pltpu.VMEM((1, 128), F32),
    la=pltpu.VMEM((NCOL, 1, 128), F32),
    lb=pltpu.VMEM((NROW, 1, 128), F32),
)
SEND = dict(load=2, t1=1, t2=1, z=1, col=1, row=1, sib=1, sg=1, rr=1, rc=1, xs=1, la=1, lb=1)
RECV = dict(t1=1, t2=1, z=3, col=QUART, row=SUPER, sib=SUPER, sg=SUPER, rr=1, rc=1, xs=2, la=1, lb=1)


def kernel(samples, scores, groups, out, *rest):
    ref = Refs(SCRATCH, rest[:len(SCRATCH)])
    sems = rest[len(SCRATCH):]
    send = Refs(SEND, sems[:len(SEND)])
    recv = Refs(RECV, sems[len(SEND):])
    row, col = lax.axis_index("row"), lax.axis_index("col")
    zh, x = row // 4, lax.rem(row, 4)
    zl, y, core = col // 16, lax.rem(col // 2, 8), lax.rem(col, 2)
    sib = col + 1 - 2 * core

    def wrap(value, size):
        return jnp.where(value >= size, value - size, value)

    barrier = pltpu.get_barrier_semaphore()

    def greet(to_row, to_col):
        pl.semaphore_signal(barrier, inc=1, device_id=(to_row, to_col), device_id_type=MESH)

    for d in FAR_ROW:
        greet(wrap(row + d, NROW), col)
    for d in FAR_COL:
        greet(row, wrap(col + d, NCOL))

    loads = [pltpu.make_async_copy(samples, ref.xin, send.load.at[0]),
             pltpu.make_async_copy(scores, ref.sin, send.load.at[1])]
    for load in loads:
        load.start()
    town = groups[0, 0].astype(F32)
    tfull = jnp.full((1, 128), town, F32)
    ref.tsrc[...] = tfull
    ref.t1[0] = tfull
    expansion(ref, row, zh, x)
    for load in loads:
        load.wait()
    own = jnp.concatenate([ref.xin[...], ref.sin[...]], axis=1)
    ref.own[...] = own
    ref.rowbuf[RG - 4] = own
    ref.colbuf[12] = own
    pl.semaphore_wait(barrier, NROW + NCOL - 2)

    def copy(src, dst, ssem, rsem, to_row, to_col):
        return pltpu.make_async_remote_copy(
            src_ref=src, dst_ref=dst, send_sem=ssem, recv_sem=rsem,
            device_id=(to_row, to_col), device_id_type=MESH,
        )

    def t1_copy(d):
        return copy(ref.tsrc, ref.t1.at[NROW - d], send.t1.at[0], recv.t1.at[0], wrap(row + d, NROW), col)

    def t2_copy(t, b):
        chip = chip_at(zl, y, OFFSETS[t], -1)
        slot = 2 * (t - 1) + lax.rem(core + b, 2)
        return copy(ref.tvec, ref.t2.at[slot], send.t2.at[0], recv.t2.at[0], row, 2 * chip + b)

    def z_copy(quarter):
        to = wrap(zh + 3 - quarter, 4) * 4 + x
        return copy(ref.own, ref.colbuf.at[quarter * 4], send.z.at[0], recv.z.at[quarter], to, col)

    def col_copy(quarter, dx):
        to = zh * 4 + wrap(x + 4 - dx, 4)
        src = ref.own if quarter == 3 else ref.colbuf.at[quarter * 4]
        return copy(src, ref.colbuf.at[quarter * 4 + dx], send.col.at[0], recv.col.at[quarter], to, col)

    def row_copy(t):
        chip = chip_at(zl, y, OFFSETS[t], -1)
        slot = GROUPS * (t // 3) + t % 3
        return copy(ref.own, ref.rowbuf.at[slot], send.row.at[0], recv.row.at[t // 3], row, 2 * chip + core)

    def sib_copy(step):
        at = GROUPS * step
        return copy(ref.rowbuf.at[at:at + 3], ref.rowbuf.at[at + 3:at + 6], send.sib.at[0], recv.sib.at[step], row, sib)

    def sg_copy(step):
        return copy(ref.sibsend.at[step], ref.sibrecv.at[step], send.sg.at[0], recv.sg.at[step], row, sib)

    def rr_copy(t):
        chip = chip_at(zl, y, OFFSETS[t], 1)
        return copy(ref.rsend.at[t], ref.rrow.at[t], send.rr.at[0], recv.rr.at[0], row, 2 * chip + core)

    def rc_copy(quarter, dx):
        src = ref.csend.at[quarter * 4 + dx]
        to_x = wrap(x + dx, 4)
        if quarter == 1:
            return copy(src, ref.rcol.at[dx], send.rc.at[0], recv.rc.at[0], wrap(zh + 2, 4) * 4 + to_x, col)
        if quarter == 3:
            return copy(src, ref.rcol.at[3 + dx], send.rc.at[0], recv.rc.at[0], zh * 4 + to_x, col)
        half = quarter // 2
        return copy(src, ref.xrecv.at[half, dx - 1], send.xs.at[0], recv.xs.at[half], zh * 4 + to_x, col)

    def zs_copy(quarter):
        to = wrap(zh + quarter + 1, 4) * 4 + x
        return copy(ref.zsend.at[quarter // 2], ref.rcol.at[7 + quarter // 2], send.rc.at[0], recv.rc.at[0], to, col)

    def la_copy(d):
        return copy(ref.lossv, ref.la.at[NCOL - d], send.la.at[0], recv.la.at[0], row, wrap(col + d, NCOL))

    def lb_copy(d):
        return copy(ref.lsum, ref.lb.at[NROW - d], send.lb.at[0], recv.lb.at[0], wrap(row + d, NROW), col)

    def landed(buf, sem):
        copy(buf, buf, sem, sem, row, sib).wait_recv()

    def left(buf, sem):
        copy(buf, buf, sem, sem, row, sib).wait_send()

    for d in FAR_ROW:
        t1_copy(d).start()
    for quarter in (1, 0, 2):
        z_copy(quarter).start()
    for t in range(CHUNKS - 1):
        row_copy(t).start()
    for dx in (2, 1, 3):
        col_copy(3, dx).start()

    def got_z(quarter):
        landed(ref.colbuf.at[quarter * 4], recv.z.at[quarter])
        for dx in (2, 1, 3):
            col_copy(quarter, dx).start()

    def got_cols(quarter):
        at = quarter * 4
        landed(ref.colbuf.at[at + 1:at + 4], recv.col.at[quarter])
        prep_cols(ref, quarter)

    def got_rows(step):
        at = GROUPS * step
        landed(ref.rowbuf.at[at:at + (2 if step == 2 else 3)], recv.row.at[step])
        sib_copy(step).start()

    def got_sib(step):
        at = GROUPS * step
        landed(ref.rowbuf.at[at + 3:at + 6], recv.sib.at[step])
        prep_rows(ref, step)

    got_z(0)
    got_z(2)
    got_rows(2)
    got_z(1)
    landed(ref.t1.at[1:NROW], recv.t1.at[0])
    lane3 = lax.broadcasted_iota(jnp.int32, (NROW, 1, 128), 2)
    slot3 = lax.broadcasted_iota(jnp.int32, (NROW, 1, 128), 0)
    ref.tvec[...] = jnp.sum(jnp.where(lane3 == slot3, ref.t1[...], 0.0), axis=0)
    for t in range(1, CHUNKS - 1):
        for b in range(2):
            t2_copy(t, b).start()
    got_rows(1)
    got_rows(0)
    got_cols(3)
    got_sib(2)
    pair_step(ref, 2, 3)
    got_cols(0)
    pair_step(ref, 2, 0)
    got_sib(1)
    pair_step(ref, 1, 3)
    pair_step(ref, 1, 0)
    got_cols(2)
    pair_step(ref, 2, 2)
    pair_step(ref, 1, 2)
    got_sib(0)
    pair_step(ref, 0, 3)
    pair_step(ref, 0, 0)
    pair_step(ref, 0, 2)
    got_cols(1)
    for step in range(SUPER):
        pair_step(ref, step, 1)
    landed(ref.t2, recv.t2.at[0])
    pair_weights(ref, town, row)

    lane = lanes()
    own32 = ref.own[...].astype(F32)
    kept_diag = jnp.where((row // 2).astype(F32) < jnp.full((1, 128), town, F32), 1.0, 0.0)
    part = jnp.zeros((1, NROW * M), F32)
    for step in range(SUPER):
        part = part + jnp.sum(ref.usum[step, 0:GROUPS] * ref.wtab[step, 0:GROUPS], axis=0, keepdims=True)
    s2 = jnp.sum(jnp.where(lane < 64, 1.0 / 64, own32 * own32), axis=0, keepdims=True)
    loss = jnp.sum(part, axis=1, keepdims=True) - jnp.sum(s2 * kept_diag, axis=1, keepdims=True)
    count = tfull * (128.0 * 2048.0) - 64.0 * kept_diag
    lossv = jnp.where(lane == 0, loss, jnp.where(lane == 1, count, 0.0))
    ref.lossv[...] = lossv
    ref.la[0] = lossv
    for d in FAR_COL:
        la_copy(d).start()

    def cols_out(quarter):
        col_results(ref, quarter)
        for dx in (2, 1, 3, 0):
            if quarter == 1 or dx:
                rc_copy(quarter, dx).start()

    def cols_on(quarter):
        half = quarter // 2
        landed(ref.xrecv.at[half], recv.xs.at[half])
        both = ref.colown[quarter] + jnp.sum(ref.xrecv[half].astype(F32), axis=0)
        ref.zsend[half] = both.astype(BF16)
        zs_copy(quarter).start()

    def rows_out(step):
        row_results(ref, step)
        sg_copy(step).start()

    def rows_on(step):
        landed(ref.sibrecv.at[step], recv.sg.at[step])
        both = ref.rowg[step] + ref.sibrecv[step]
        if step == SUPER - 1:
            ref.rsend[6:8] = both[0:2].astype(BF16)
            ref.rowown[...] = both[2]
        else:
            ref.rsend[3 * step:3 * step + 3] = both.astype(BF16)
        for t in range(3 * step, min(3 * step + 3, CHUNKS - 1)):
            rr_copy(t).start()

    rows_out(0)
    cols_out(0)
    cols_out(2)
    cols_out(1)
    rows_on(0)
    rows_out(1)
    rows_out(2)
    cols_out(3)
    rows_on(1)
    rows_on(2)
    landed(ref.la.at[1:NCOL], recv.la.at[0])
    lsum = jnp.sum(ref.la[...], axis=0)
    ref.lsum[...] = lsum
    ref.lb[0] = lsum
    for d in FAR_ROW:
        lb_copy(d).start()
    cols_on(0)
    cols_on(2)

    total = ref.rowown[...] + ref.colown[3] - jnp.where(lane < 64, 0.0, 2.0 * kept_diag * own32)
    landed(ref.rrow, recv.rr.at[0])
    total = total + jnp.sum(ref.rrow[...].astype(F32), axis=0)
    landed(ref.rcol, recv.rc.at[0])
    total = total + jnp.sum(ref.rcol[...].astype(F32), axis=0)

    landed(ref.lb.at[1:NROW], recv.lb.at[0])
    sums = jnp.sum(ref.lb[...], axis=0)
    pairs = sums[:, 1:2]
    out[0:64, :] = total * (EVERYONE / pairs)
    out[64:72, :] = jnp.broadcast_to(sums[:, 0:1] / pairs, (8, 128))

    left(ref.t1.at[1:NROW], send.t1.at[0])
    left(ref.t2, send.t2.at[0])
    left(ref.colbuf.at[0:3], send.z.at[0])
    left(ref.colbuf.at[0:12], send.col.at[0])
    left(ref.rrow, send.row.at[0])
    left(ref.rowbuf.at[0:CHUNKS], send.sib.at[0])
    left(ref.sibsend, send.sg.at[0])
    left(ref.rrow, send.rr.at[0])
    left(ref.rcol, send.rc.at[0])
    left(ref.xrecv, send.xs.at[0])
    left(ref.la.at[1:NCOL], send.la.at[0])
    left(ref.lb.at[1:NROW], send.lb.at[0])


def shards(samples, scores, tile_groups):
    vmem = pl.BlockSpec(memory_space=pltpu.VMEM)
    hbm = pl.BlockSpec(memory_space=pltpu.HBM)
    out = pl.pallas_call(
        kernel,
        out_shape=jax.ShapeDtypeStruct((M + 8, 128), F32),
        in_specs=[hbm, hbm, pl.BlockSpec(memory_space=pltpu.SMEM)],
        out_specs=vmem,
        scratch_shapes=list(SCRATCH.values())
        + [pltpu.SemaphoreType.DMA((n,)) for n in (*SEND.values(), *RECV.values())],
        compiler_params=pltpu.CompilerParams(
            collective_id=0, has_side_effects=True, vmem_limit_bytes=64 * 2**20
        ),
    )(samples, scores, tile_groups)
    def split(whole, out_x, out_s, out_loss):
        out_x[...] = whole[0:M, 0:64]
        out_s[...] = whole[0:M, 64:128]
        out_loss[...] = whole[M:M + 1, 0:1]

    out_x, out_s, loss = pl.pallas_call(
        split,
        out_shape=(
            jax.ShapeDtypeStruct((M, 64), F32),
            jax.ShapeDtypeStruct((M, 64), F32),
            jax.ShapeDtypeStruct((1, 1), F32),
        ),
        in_specs=[vmem],
        out_specs=(vmem, vmem, vmem),
        compiler_params=pltpu.CompilerParams(vmem_limit_bytes=64 * 2**20),
    )(out)
    return out_x, out_s, loss[0, 0]


def solution(mesh):
    placed = (P(("row", "col"), None), P(("row", "col"), None), P("row", "col"))
    return jax.shard_map(
        shards,
        mesh=mesh,
        in_specs=placed,
        out_specs=(P(("row", "col"), None), P(("row", "col"), None), P()),
        check_vma=False,
    )
```

```python
import jax
import jax.numpy as jnp
from jax import lax
from jax.experimental import pallas as pl
from jax.experimental.pallas import tpu as pltpu
from jax.sharding import PartitionSpec as P

MESH = pl.DeviceIdType.MESH
F32 = jnp.float32
BF16 = jnp.bfloat16

NROW, NCOL = 16, 32
M = 64
CHUNKS = 9
RG = 2 * CHUNKS
SUPER = 3
GROUPS = RG // SUPER
ROWS = GROUPS * M
QUART = 4
QCOLS = 4 * M
EVERYONE = float(M * NROW * NCOL)
FAR_ROW = (10, 8, 9, 11, 6, 14, 4, 12, 5, 7, 13, 15, 2, 1, 3)
FAR_COL = tuple(sorted(range(1, 32), key=lambda d: -min((d // 2) % 8, 8 - (d // 2) % 8)))
NSLOT = 14

OFFSETS = (
    (0, 4, True), (0, 3, False), (1, -3, False),
    (1, None, False), (1, 2, False), (0, -2, False),
    (0, 1, False), (1, -1, False), (0, 0, True),
)


def split3(value):
    hi = value.astype(BF16).astype(F32)
    rest = value - hi
    mid = rest.astype(BF16).astype(F32)
    return hi, mid, rest - mid


def dot(a, b):
    return lax.dot_general(a, b, (((1,), (0,)), ((), ())), preferred_element_type=F32)


def dot_nt(a, b):
    return lax.dot_general(a, b, (((1,), (1,)), ((), ())), preferred_element_type=F32)


def lanes(rows=1, width=128):
    return lax.broadcasted_iota(jnp.int32, (rows, width), 1)


def squares(p, sw):
    q = p * jnp.where(lanes() < 64, p, sw)
    hi = q.astype(BF16)
    return jnp.concatenate([hi, (q - hi.astype(F32)).astype(BF16)], axis=1)


def sum_weights(e_lanes, s_lanes):
    k = lax.broadcasted_iota(jnp.int32, (256, 128), 0) % 128
    lane = lax.broadcasted_iota(jnp.int32, (256, 128), 1)
    is_x = k < 64
    out = jnp.zeros((256, 128), F32)
    if e_lanes is not None:
        in_e = (lane >= e_lanes) & (lane < e_lanes + 3)
        out = jnp.where(in_e & is_x, -(2.0 ** -7), out)
    if s_lanes is not None:
        in_s = (lane >= s_lanes) & (lane < s_lanes + 3)
        out = jnp.where(in_s, jnp.where(is_x, -(2.0 ** -18), 2.0 ** -12), out)
    return out.astype(BF16)


def pick3(value):
    hi, mid, lo = split3(value)
    part = lanes() % 3
    return jnp.where(part == 0, hi, jnp.where(part == 1, mid, lo))


def prep_rows(ref, step):
    pair = ref.rowbuf[pl.ds(step * GROUPS, GROUPS)].reshape(ROWS, 128)
    p = pair.astype(F32)
    sw = pltpu.roll(p, 64, 1)
    lane = lanes()
    sums = dot(squares(p, sw), sum_weights(0, 6))
    one = (((lane >= 3) & (lane < 6)) | (lane == 9)).astype(F32)
    misc = pick3(sums) + one
    ext = jnp.where(lane < 64, misc, p).astype(BF16)
    ref.a_op[step] = jnp.concatenate([pair, ext], axis=1)
    pt = p.T
    xt, st = pt[0:64], pt[64:128]
    ones = jnp.ones((16, ROWS), F32)
    at = pl.ds(step * ROWS, ROWS)
    ref.f1t[:, at] = jnp.concatenate([st * (-1.0 / 64), st, xt * (-1.0 / 64), ones], axis=0).astype(BF16)
    ref.f2t[:, at] = jnp.concatenate([xt, ones], axis=0).astype(BF16)


def prep_cols(ref, quarter):
    pair = ref.colbuf[pl.ds(quarter * 4, 4)].reshape(QCOLS, 128)
    p = pair.astype(F32)
    sw = pltpu.roll(p, 64, 1)
    lane = lanes()
    first = lane < 64
    sq = squares(p, sw)
    sums_e = dot(sq, sum_weights(3, None))
    sums_s = dot(sq, sum_weights(None, 3))
    u = p * jnp.where(first, 2.0 ** -17, 2.0 ** -6) - sw * (2.0 ** -12)
    u_hi = u.astype(BF16)
    e1 = jnp.where(first, p * (1.0 / 64), 0.0).astype(BF16)
    e2 = pick3(sums_e) + (lane < 3).astype(F32)
    s2 = pick3(sums_s) + ((lane >= 6) & (lane < 9)).astype(F32) + jnp.where(lane == 9, 33.0 / 2048, 0.0)
    s2 = jnp.where(first, s2, u - u_hi.astype(F32))
    ref.b_op[quarter, 0:QCOLS, :] = jnp.concatenate([e1, e2.astype(BF16)], axis=1)
    ref.b_op[quarter, QCOLS:2 * QCOLS, :] = jnp.concatenate([u_hi, s2.astype(BF16)], axis=1)
    sw64 = sw * (-1.0 / 64)
    f1a = jnp.where(first, sw64, p)
    f1b = jnp.where(first, (lane == 0).astype(F32), sw64)
    f2a = jnp.where(first, p, 0.0)
    f2b = jnp.broadcast_to((lane == 1).astype(F32), p.shape)
    at = pl.ds(quarter * QCOLS, QCOLS)
    ref.f1[at, :] = jnp.concatenate([f1a, f1b], axis=1).astype(BF16)
    ref.f2[at, :] = jnp.concatenate([f2a, f2b], axis=1).astype(BF16)
    ref.colt[quarter] = p.T


def pair_step(ref, step, quarter):
    es = dot_nt(ref.a_op[step], ref.b_op[quarter])
    kept = jnp.exp(es[:, :QCOLS])
    coef = kept * es[:, QCOLS:]
    at = (pl.ds(step * ROWS, ROWS), slice(quarter * QCOLS, (quarter + 1) * QCOLS))
    ref.kmat[at] = kept.astype(BF16)
    ref.cmat[at] = coef.astype(BF16)
    to = (step, slice(0, GROUPS), slice(quarter * QCOLS, (quarter + 1) * QCOLS))
    ref.usum[to] = jnp.sum((coef * 64.0 - kept * (1.0 / 32)).reshape(GROUPS, M, QCOLS), axis=1)


def expansion(ref, row, zh, x):
    lane = lanes(1, NROW * M)
    slot = lane // M
    quarter, dx = slot // 4, slot % 4
    other = ((zh + quarter + 1) % 4) * 4 + (x + dx) % 4
    place = (other - row + NROW) % NROW
    hot = (lax.broadcasted_iota(jnp.int32, (NROW, NROW * M), 0) == place).astype(F32)
    ref.spread[...] = jnp.concatenate([hot, jnp.zeros((128 - NROW, NROW * M), F32)], axis=0).astype(BF16)


def pair_weights(ref, town, row):
    lane = lanes()
    theirs = ((row + lane) % NROW) // 2
    k12 = (theirs.astype(F32) < town).astype(F32)
    half = (row // 2).astype(F32)
    ref.table[...] = jnp.zeros_like(ref.table)
    for step in range(SUPER):
        for i in range(GROUPS):
            rel, t = i // 3, 3 * step + i % 3
            weight = k12
            if not OFFSETS[t][2]:
                weight = k12 + (half < ref.t2[2 * (t - 1) + rel]).astype(F32)
            ref.table[8 * step + i:8 * step + i + 1, :] = weight
    ref.wtab[...] = dot(ref.table[...].astype(BF16), ref.spread[...]).reshape(4, 8, NROW * M)


def weighted(mat, ref, step, start, width):
    at = slice(start, start + width)
    out = []
    for i in range(GROUPS):
        w = jnp.broadcast_to(ref.wtab[step, i:i + 1, at], (16, width)).astype(BF16)
        part = mat[step * ROWS + i * M:step * ROWS + (i + 1) * M, at]
        out.append(part * jnp.concatenate([w] * (M // 16), axis=0))
    return jnp.concatenate(out, axis=0)


def row_results(ref, step):
    kb = weighted(ref.kmat, ref, step, 0, NROW * M)
    cb = weighted(ref.cmat, ref, step, 0, NROW * M)
    acc = dot(kb, ref.f1[...]) + dot(cb, ref.f2[...])
    low, high = acc[:, :128], acc[:, 128:]
    ks, cs = high[:, 0:1], high[:, 1:2]
    p = ref.rowbuf[step * GROUPS:(step + 1) * GROUPS].reshape(ROWS, 128).astype(F32)
    sw = pltpu.roll(p, 64, 1)
    grad = low + jnp.where(lanes() < 64, p * (-cs), high) + sw * (ks * (1.0 / 64))
    grad = grad.reshape(GROUPS, M, 128)
    ref.rowg[step] = grad[0:3]
    ref.sibsend[step] = grad[3:6]


def col_results(ref, quarter):
    kb = jnp.concatenate([weighted(ref.kmat, ref, s, quarter * QCOLS, QCOLS) for s in range(SUPER)], axis=0)
    cb = jnp.concatenate([weighted(ref.cmat, ref, s, quarter * QCOLS, QCOLS) for s in range(SUPER)], axis=0)
    g1 = dot(ref.f1t[...], kb)
    g2 = dot(ref.f2t[...], cb)
    pt = ref.colt[quarter]
    xt, st = pt[0:64], pt[64:128]
    ks = g1[192:193] * (1.0 / 64)
    cs = g2[64:65]
    gx = g2[0:64] + g1[0:64] - xt * cs + st * ks
    gs = g1[64:128] + g1[128:192] + xt * ks
    grad = jnp.concatenate([gx, gs], axis=0).T.reshape(4, M, 128)
    ref.csend[quarter * 4:quarter * 4 + 4] = grad.astype(BF16)
    ref.colown[quarter] = grad[0]


def chip_at(zl, y, offset, sign):
    other, dy, _ = offset
    z = lax.rem(zl + other, 2)
    if dy is None:
        from_z = zl if sign > 0 else z
        dy = 4 * from_z
    return z * 8 + lax.rem(y + sign * dy + 16, 8)


class Refs:
    def __init__(self, names, refs):
        for name, r in zip(names, refs):
            setattr(self, name, r)


SCRATCH = dict(
    xin=pltpu.VMEM((M, 64), BF16),
    sin=pltpu.VMEM((M, 64), BF16),
    own=pltpu.VMEM((M, 128), BF16),
    rowbuf=pltpu.VMEM((RG, M, 128), BF16),
    colbuf=pltpu.VMEM((NROW, M, 128), BF16),
    t1=pltpu.VMEM((NROW, 1, 128), F32),
    t2=pltpu.VMEM((NSLOT, 1, 128), F32),
    tsrc=pltpu.VMEM((1, 128), F32),
    tvec=pltpu.VMEM((1, 128), F32),
    table=pltpu.VMEM((32, 128), F32),
    spread=pltpu.VMEM((128, NROW * M), BF16),
    wtab=pltpu.VMEM((4, 8, NROW * M), F32),
    a_op=pltpu.VMEM((SUPER, ROWS, 256), BF16),
    b_op=pltpu.VMEM((QUART, 2 * QCOLS, 256), BF16),
    f1=pltpu.VMEM((NROW * M, 256), BF16),
    f2=pltpu.VMEM((NROW * M, 256), BF16),
    f1t=pltpu.VMEM((208, RG * M), BF16),
    f2t=pltpu.VMEM((80, RG * M), BF16),
    colt=pltpu.VMEM((QUART, 128, QCOLS), F32),
    kmat=pltpu.VMEM((RG * M, NROW * M), BF16),
    cmat=pltpu.VMEM((RG * M, NROW * M), BF16),
    usum=pltpu.VMEM((SUPER, 8, NROW * M), F32),
    rowg=pltpu.VMEM((SUPER, 3, M, 128), F32),
    sibsend=pltpu.VMEM((SUPER, 3, M, 128), F32),
    sibrecv=pltpu.VMEM((SUPER, 3, M, 128), F32),
    rsend=pltpu.VMEM((CHUNKS - 1, M, 128), BF16),
    csend=pltpu.VMEM((NROW, M, 128), BF16),
    rowown=pltpu.VMEM((M, 128), F32),
    colown=pltpu.VMEM((QUART, M, 128), F32),
    xrecv=pltpu.VMEM((2, 3, M, 128), BF16),
    zsend=pltpu.VMEM((2, M, 128), BF16),
    rrow=pltpu.VMEM((CHUNKS - 1, M, 128), BF16),
    rcol=pltpu.VMEM((9, M, 128), BF16),
    lossv=pltpu.VMEM((1, 128), F32),
    lsum=pltpu.VMEM((1, 128), F32),
    la=pltpu.VMEM((NCOL, 1, 128), F32),
    lb=pltpu.VMEM((NROW, 1, 128), F32),
)
SEND = dict(load=2, t1=1, t2=1, z=1, col=1, row=1, sib=1, sg=1, rr=1, rc=1, xs=1, la=1, lb=1)
RECV = dict(t1=1, t2=1, z=3, col=QUART, row=SUPER, sib=SUPER, sg=SUPER, rr=1, rc=1, xs=2, la=1, lb=1)


def kernel(samples, scores, groups, out, *rest):
    ref = Refs(SCRATCH, rest[:len(SCRATCH)])
    sems = rest[len(SCRATCH):]
    send = Refs(SEND, sems[:len(SEND)])
    recv = Refs(RECV, sems[len(SEND):])
    row, col = lax.axis_index("row"), lax.axis_index("col")
    zh, x = row // 4, lax.rem(row, 4)
    zl, y, core = col // 16, lax.rem(col // 2, 8), lax.rem(col, 2)
    sib = col + 1 - 2 * core

    def wrap(value, size):
        return jnp.where(value >= size, value - size, value)

    barrier = pltpu.get_barrier_semaphore()

    def greet(to_row, to_col):
        pl.semaphore_signal(barrier, inc=1, device_id=(to_row, to_col), device_id_type=MESH)

    for d in FAR_ROW:
        greet(wrap(row + d, NROW), col)
    for d in FAR_COL:
        greet(row, wrap(col + d, NCOL))

    loads = [pltpu.make_async_copy(samples, ref.xin, send.load.at[0]),
             pltpu.make_async_copy(scores, ref.sin, send.load.at[1])]
    for load in loads:
        load.start()
    town = groups[0, 0].astype(F32)
    tfull = jnp.full((1, 128), town, F32)
    ref.tsrc[...] = tfull
    ref.t1[0] = tfull
    expansion(ref, row, zh, x)
    for load in loads:
        load.wait()
    own = jnp.concatenate([ref.xin[...], ref.sin[...]], axis=1)
    ref.own[...] = own
    ref.rowbuf[RG - 4] = own
    ref.colbuf[12] = own
    pl.semaphore_wait(barrier, NROW + NCOL - 2)

    def copy(src, dst, ssem, rsem, to_row, to_col):
        return pltpu.make_async_remote_copy(
            src_ref=src, dst_ref=dst, send_sem=ssem, recv_sem=rsem,
            device_id=(to_row, to_col), device_id_type=MESH,
        )

    def t1_copy(d):
        return copy(ref.tsrc, ref.t1.at[NROW - d], send.t1.at[0], recv.t1.at[0], wrap(row + d, NROW), col)

    def t2_copy(t, b):
        chip = chip_at(zl, y, OFFSETS[t], -1)
        slot = 2 * (t - 1) + lax.rem(core + b, 2)
        return copy(ref.tvec, ref.t2.at[slot], send.t2.at[0], recv.t2.at[0], row, 2 * chip + b)

    def z_copy(quarter):
        to = wrap(zh + 3 - quarter, 4) * 4 + x
        return copy(ref.own, ref.colbuf.at[quarter * 4], send.z.at[0], recv.z.at[quarter], to, col)

    def col_copy(quarter, dx):
        to = zh * 4 + wrap(x + 4 - dx, 4)
        src = ref.own if quarter == 3 else ref.colbuf.at[quarter * 4]
        return copy(src, ref.colbuf.at[quarter * 4 + dx], send.col.at[0], recv.col.at[quarter], to, col)

    def row_copy(t):
        chip = chip_at(zl, y, OFFSETS[t], -1)
        slot = GROUPS * (t // 3) + t % 3
        return copy(ref.own, ref.rowbuf.at[slot], send.row.at[0], recv.row.at[t // 3], row, 2 * chip + core)

    def sib_copy(step):
        at = GROUPS * step
        return copy(ref.rowbuf.at[at:at + 3], ref.rowbuf.at[at + 3:at + 6], send.sib.at[0], recv.sib.at[step], row, sib)

    def sg_copy(step):
        return copy(ref.sibsend.at[step], ref.sibrecv.at[step], send.sg.at[0], recv.sg.at[step], row, sib)

    def rr_copy(t):
        chip = chip_at(zl, y, OFFSETS[t], 1)
        return copy(ref.rsend.at[t], ref.rrow.at[t], send.rr.at[0], recv.rr.at[0], row, 2 * chip + core)

    def rc_copy(quarter, dx):
        src = ref.csend.at[quarter * 4 + dx]
        to_x = wrap(x + dx, 4)
        if quarter == 1:
            return copy(src, ref.rcol.at[dx], send.rc.at[0], recv.rc.at[0], wrap(zh + 2, 4) * 4 + to_x, col)
        if quarter == 3:
            return copy(src, ref.rcol.at[3 + dx], send.rc.at[0], recv.rc.at[0], zh * 4 + to_x, col)
        half = quarter // 2
        return copy(src, ref.xrecv.at[half, dx - 1], send.xs.at[0], recv.xs.at[half], zh * 4 + to_x, col)

    def zs_copy(quarter):
        to = wrap(zh + quarter + 1, 4) * 4 + x
        return copy(ref.zsend.at[quarter // 2], ref.rcol.at[7 + quarter // 2], send.rc.at[0], recv.rc.at[0], to, col)

    def la_copy(d):
        return copy(ref.lossv, ref.la.at[NCOL - d], send.la.at[0], recv.la.at[0], row, wrap(col + d, NCOL))

    def lb_copy(d):
        return copy(ref.lsum, ref.lb.at[NROW - d], send.lb.at[0], recv.lb.at[0], wrap(row + d, NROW), col)

    def landed(buf, sem):
        copy(buf, buf, sem, sem, row, sib).wait_recv()

    def left(buf, sem):
        copy(buf, buf, sem, sem, row, sib).wait_send()

    for d in FAR_ROW:
        t1_copy(d).start()
    for quarter in (1, 0, 2):
        z_copy(quarter).start()
    for t in range(CHUNKS - 1):
        row_copy(t).start()
    for dx in (2, 1, 3):
        col_copy(3, dx).start()

    def got_z(quarter):
        landed(ref.colbuf.at[quarter * 4], recv.z.at[quarter])
        for dx in (2, 1, 3):
            col_copy(quarter, dx).start()

    def got_cols(quarter):
        at = quarter * 4
        landed(ref.colbuf.at[at + 1:at + 4], recv.col.at[quarter])
        prep_cols(ref, quarter)

    def got_rows(step):
        at = GROUPS * step
        landed(ref.rowbuf.at[at:at + (2 if step == 2 else 3)], recv.row.at[step])
        sib_copy(step).start()

    def got_sib(step):
        at = GROUPS * step
        landed(ref.rowbuf.at[at + 3:at + 6], recv.sib.at[step])
        prep_rows(ref, step)

    got_z(0)
    got_z(2)
    got_rows(2)
    got_z(1)
    landed(ref.t1.at[1:NROW], recv.t1.at[0])
    lane3 = lax.broadcasted_iota(jnp.int32, (NROW, 1, 128), 2)
    slot3 = lax.broadcasted_iota(jnp.int32, (NROW, 1, 128), 0)
    ref.tvec[...] = jnp.sum(jnp.where(lane3 == slot3, ref.t1[...], 0.0), axis=0)
    for t in range(1, CHUNKS - 1):
        for b in range(2):
            t2_copy(t, b).start()
    got_rows(1)
    got_rows(0)
    got_cols(3)
    got_sib(2)
    pair_step(ref, 2, 3)
    got_cols(0)
    pair_step(ref, 2, 0)
    got_sib(1)
    pair_step(ref, 1, 3)
    pair_step(ref, 1, 0)
    got_cols(2)
    pair_step(ref, 2, 2)
    pair_step(ref, 1, 2)
    got_sib(0)
    pair_step(ref, 0, 3)
    pair_step(ref, 0, 0)
    pair_step(ref, 0, 2)
    got_cols(1)
    for step in range(SUPER):
        pair_step(ref, step, 1)
    landed(ref.t2, recv.t2.at[0])
    pair_weights(ref, town, row)

    lane = lanes()
    own32 = ref.own[...].astype(F32)
    kept_diag = jnp.where((row // 2).astype(F32) < jnp.full((1, 128), town, F32), 1.0, 0.0)
    part = jnp.zeros((1, NROW * M), F32)
    for step in range(SUPER):
        part = part + jnp.sum(ref.usum[step, 0:GROUPS] * ref.wtab[step, 0:GROUPS], axis=0, keepdims=True)
    s2 = jnp.sum(jnp.where(lane < 64, 1.0 / 64, own32 * own32), axis=0, keepdims=True)
    loss = jnp.sum(part, axis=1, keepdims=True) - jnp.sum(s2 * kept_diag, axis=1, keepdims=True)
    count = tfull * (128.0 * 2048.0) - 64.0 * kept_diag
    lossv = jnp.where(lane == 0, loss, jnp.where(lane == 1, count, 0.0))
    ref.lossv[...] = lossv
    ref.la[0] = lossv
    for d in FAR_COL:
        la_copy(d).start()

    def cols_out(quarter):
        col_results(ref, quarter)
        for dx in (2, 1, 3, 0):
            if quarter == 1 or dx:
                rc_copy(quarter, dx).start()

    def cols_on(quarter):
        half = quarter // 2
        landed(ref.xrecv.at[half], recv.xs.at[half])
        both = ref.colown[quarter] + jnp.sum(ref.xrecv[half].astype(F32), axis=0)
        ref.zsend[half] = both.astype(BF16)
        zs_copy(quarter).start()

    def rows_out(step):
        row_results(ref, step)
        sg_copy(step).start()

    def rows_on(step):
        landed(ref.sibrecv.at[step], recv.sg.at[step])
        both = ref.rowg[step] + ref.sibrecv[step]
        if step == SUPER - 1:
            ref.rsend[6:8] = both[0:2].astype(BF16)
            ref.rowown[...] = both[2]
        else:
            ref.rsend[3 * step:3 * step + 3] = both.astype(BF16)
        for t in range(3 * step, min(3 * step + 3, CHUNKS - 1)):
            rr_copy(t).start()

    rows_out(0)
    cols_out(0)
    cols_out(2)
    cols_out(1)
    rows_on(0)
    rows_out(1)
    rows_out(2)
    cols_out(3)
    rows_on(1)
    landed(ref.la.at[1:NCOL], recv.la.at[0])
    lsum = jnp.sum(ref.la[...], axis=0)
    ref.lsum[...] = lsum
    ref.lb[0] = lsum
    for d in FAR_ROW:
        lb_copy(d).start()
    rows_on(2)
    cols_on(0)
    cols_on(2)

    total = ref.rowown[...] + ref.colown[3] - jnp.where(lane < 64, 0.0, 2.0 * kept_diag * own32)
    landed(ref.rrow, recv.rr.at[0])
    total = total + jnp.sum(ref.rrow[...].astype(F32), axis=0)
    landed(ref.rcol, recv.rc.at[0])
    total = total + jnp.sum(ref.rcol[...].astype(F32), axis=0)

    landed(ref.lb.at[1:NROW], recv.lb.at[0])
    sums = jnp.sum(ref.lb[...], axis=0)
    pairs = sums[:, 1:2]
    out[0:64, :] = total * (EVERYONE / pairs)
    out[64:72, :] = jnp.broadcast_to(sums[:, 0:1] / pairs, (8, 128))

    left(ref.t1.at[1:NROW], send.t1.at[0])
    left(ref.t2, send.t2.at[0])
    left(ref.colbuf.at[0:3], send.z.at[0])
    left(ref.colbuf.at[0:12], send.col.at[0])
    left(ref.rrow, send.row.at[0])
    left(ref.rowbuf.at[0:CHUNKS], send.sib.at[0])
    left(ref.sibsend, send.sg.at[0])
    left(ref.rrow, send.rr.at[0])
    left(ref.rcol, send.rc.at[0])
    left(ref.xrecv, send.xs.at[0])
    left(ref.la.at[1:NCOL], send.la.at[0])
    left(ref.lb.at[1:NROW], send.lb.at[0])


def shards(samples, scores, tile_groups):
    vmem = pl.BlockSpec(memory_space=pltpu.VMEM)
    hbm = pl.BlockSpec(memory_space=pltpu.HBM)
    out = pl.pallas_call(
        kernel,
        out_shape=jax.ShapeDtypeStruct((M + 8, 128), F32),
        in_specs=[hbm, hbm, pl.BlockSpec(memory_space=pltpu.SMEM)],
        out_specs=vmem,
        scratch_shapes=list(SCRATCH.values())
        + [pltpu.SemaphoreType.DMA((n,)) for n in (*SEND.values(), *RECV.values())],
        compiler_params=pltpu.CompilerParams(
            collective_id=0, has_side_effects=True, vmem_limit_bytes=64 * 2**20
        ),
    )(samples, scores, tile_groups)
    def split(whole, out_x, out_s, out_loss):
        out_x[...] = whole[0:M, 0:64]
        out_s[...] = whole[0:M, 64:128]
        out_loss[...] = whole[M:M + 1, 0:1]

    out_x, out_s, loss = pl.pallas_call(
        split,
        out_shape=(
            jax.ShapeDtypeStruct((M, 64), F32),
            jax.ShapeDtypeStruct((M, 64), F32),
            jax.ShapeDtypeStruct((1, 1), F32),
        ),
        in_specs=[vmem],
        out_specs=(vmem, vmem, vmem),
        compiler_params=pltpu.CompilerParams(vmem_limit_bytes=64 * 2**20),
    )(out)
    return out_x, out_s, loss[0, 0]


def solution(mesh):
    placed = (P(("row", "col"), None), P(("row", "col"), None), P("row", "col"))
    return jax.shard_map(
        shards,
        mesh=mesh,
        in_specs=placed,
        out_specs=(P(("row", "col"), None), P(("row", "col"), None), P()),
        check_vma=False,
    )
```
